32 devices in a mesh: clip: 4 (over y, x), seq: 8 (over z, core).
Axes of the slice: x: 2, y: 2, z: 4, core: 2. Of those that a mesh axis runs over, the one named last changes fastest.
Arguments:
- frames_in: bfloat16 [128, 64, 1152], P(('clip', 'seq')), parts along dimension 0, may hold values from -6 to 6
- modulation: float32 [12, 1152], P('clip'), parts along dimension 0, may hold values from -3 to 3
- self_proj: bfloat16 [1152, 1728], P(None, 'seq'), may hold values from -0.1875 to 0.1875
- self_out: bfloat16 [576, 1152], P(None, 'seq'), may hold values from -0.25 to 0.25
- cross_query: bfloat16 [1152, 576], P(None, 'seq'), may hold values from -0.1875 to 0.1875
- cross_keyval: bfloat16 [1152, 1152], P(None, 'seq'), may hold values from -0.1875 to 0.1875
- cross_out: bfloat16 [576, 1152], P(None, 'seq'), may hold values from -0.25 to 0.25
- text_bank: bfloat16 [8, 256, 1152], P('seq'), may hold values from -6 to 6
- prompt_pick: int32 [4], P('clip'), parts along dimension 0, may hold values from 0 to 7
- text_lengths: int32 [8], replicated, may hold values from 32 to 256
Outputs:
- frames_out: bfloat16 [128, 64, 1152], P(('clip', 'seq')), parts along dimension 0
The draws below stay inside these ranges and needn't reach their ends.
There are 4 independent parts, one for each index of `clip`. The reference program is written for one: setup_inputs(seed, part) draws one part's arguments, and reference() takes and returns one part's arrays. A program takes and returns all parts, laid end to end along the dimension named above; an argument that names none is the same for every part. Nothing has to cross between parts.
All inputs are finite; a program needn't handle non-finite values.
Results may differ from the reference program's by a relative error of at most 0.006.
Values may be sent and summed in bfloat16 or wider, within the bound.
A program may use at most 64 MiB of HBM per device.

```python
import math
import jax
import jax.numpy as jnp
from jax import lax

WIDTH = 1152
HEAD_DIM = 72
HEADS_WIN = 8
ATTN = 576
FRAMES = 32
PIXELS = 64
TXT = 256
PROMPTS = 8


def set_ends(result, own_key, smallest, high):
    longest = result.shape.index(max(result.shape))
    spots = []
    for shift in (0, 1):
        where = [jax.random.randint(jax.random.fold_in(own_key, axis), (), 0, length) for axis, length in enumerate(result.shape)]
        where[longest] = (where[longest] + shift) % result.shape[longest]
        spots.append(tuple(where))
    return result.at[spots[0]].set(smallest).at[spots[1]].set(high)


def level_of(own_key, dims, split, least, top_value):
    def one(dim, parts):
        heights = jax.random.uniform(jax.random.fold_in(jax.random.fold_in(own_key, 6), dim), (parts,), jnp.float32, least / len(split), top_value / len(split))
        return jnp.repeat(jnp.exp(heights), dims[dim] // parts).reshape((-1,) + (1,) * (len(dims) - dim - 1))

    loudness = one(*split[0])
    for cut in split[1:]:
        loudness = loudness * one(*cut)
    return loudness


def noise(own_key, shape, scale, bound, cuts=(), kind=jnp.bfloat16):
    factor_of = level_of(own_key, shape, cuts, -0.22, 0.18) if cuts else 1.0
    entries = jax.random.normal(own_key, shape, jnp.float32) * scale * factor_of
    return jnp.minimum(jnp.maximum(entries, -bound), bound).astype(kind)


def setup_inputs(seed: int = 0, part: int = 0) -> dict:
    splits = jax.random.split(jax.random.key(seed), 11)
    own_keys = jax.random.split(jax.random.fold_in(splits[10], part), 11)
    return {
        "frames_in": noise(own_keys[0], (FRAMES, PIXELS, WIDTH), 1.0, 6.0, ((0, 8),)),
        "modulation": noise(own_keys[1], (3, WIDTH), 0.5, 3.0, (), jnp.float32),
        "self_proj": noise(splits[2], (WIDTH, 3 * ATTN), WIDTH ** -0.5, 0.1875, ((1, 8),)),
        "self_out": noise(splits[3], (ATTN, WIDTH), ATTN ** -0.5, 0.25, ((1, 8),)),
        "cross_query": noise(splits[4], (WIDTH, ATTN), WIDTH ** -0.5, 0.1875, ((1, 8),)),
        "cross_keyval": noise(splits[5], (WIDTH, 2 * ATTN), WIDTH ** -0.5, 0.1875, ((1, 8),)),
        "cross_out": noise(splits[6], (ATTN, WIDTH), ATTN ** -0.5, 0.25, ((1, 8),)),
        "text_bank": noise(splits[7], (PROMPTS, TXT, WIDTH), 1.0, 6.0, ((0, 8),)),
        "prompt_pick": jax.random.randint(own_keys[8], (1,), 0, PROMPTS).astype(jnp.int32),
        "text_lengths": set_ends(jax.random.randint(splits[9], (PROMPTS,), TXT // 8, TXT + 1), jax.random.fold_in(splits[9], 1), TXT // 8, TXT).astype(jnp.int32),
    }


EPS = 1e-06

def layer_norm(values):
    mean = lax.optimization_barrier(jnp.mean(values, axis=-1, keepdims=True))
    centred = values - mean
    spread = lax.optimization_barrier(jnp.mean(centred * centred, axis=-1, keepdims=True))
    return centred * lax.rsqrt(spread + EPS)

def head_norm(values, heads):
    shaped = values.reshape(values.shape[:-1] + (heads, values.shape[-1] // heads))
    power = lax.optimization_barrier(jnp.mean(shaped * shaped, axis=-1, keepdims=True))
    return shaped * lax.rsqrt(power + EPS)

def reference(frames_in, modulation, self_proj, self_out, cross_query, cross_keyval, cross_out, text_bank, prompt_pick, text_lengths):
    heads = HEADS_WIN
    attn = heads * HEAD_DIM
    scale_q = 1.0 / math.sqrt(HEAD_DIM)
    tokens = frames_in.astype(jnp.float32)
    normed = (layer_norm(tokens) * (1.0 + modulation[1]) + modulation[0]).astype(jnp.bfloat16)
    qkv = jnp.dot(normed.reshape(-1, WIDTH), self_proj, preferred_element_type=jnp.float32).astype(jnp.bfloat16)
    qkv = qkv.reshape(FRAMES, PIXELS, 3 * attn)
    query = (head_norm(qkv[..., :attn].astype(jnp.float32), heads) * scale_q).astype(jnp.bfloat16)
    key = head_norm(qkv[..., attn:2 * attn].astype(jnp.float32), heads).astype(jnp.bfloat16)
    value = qkv[..., 2 * attn:].reshape(FRAMES, PIXELS, heads, HEAD_DIM)
    scores = jnp.einsum('fphd,gphd->phfg', query.astype(jnp.float32), key.astype(jnp.float32))
    weights = jnp.exp(scores)
    total = lax.optimization_barrier(jnp.sum(weights, axis=-1))
    probs = lax.optimization_barrier(weights.astype(jnp.bfloat16)).astype(jnp.float32)
    mixed = jnp.einsum('phfg,gphd->fphd', probs, value.astype(jnp.float32))
    attended = (mixed / jnp.transpose(total, (2, 0, 1))[..., None]).astype(jnp.bfloat16).reshape(-1, attn)
    self_term = jnp.dot(attended, self_out, preferred_element_type=jnp.float32)
    after_self = (tokens.reshape(-1, WIDTH) + modulation[2] * self_term).astype(jnp.bfloat16)
    pick = prompt_pick[0]
    memory = lax.dynamic_index_in_dim(text_bank, pick, 0, keepdims=False)
    keyval = jnp.dot(memory, cross_keyval, preferred_element_type=jnp.float32).astype(jnp.bfloat16)
    text_key = head_norm(keyval[:, :attn].astype(jnp.float32), heads).astype(jnp.bfloat16)
    text_value = keyval[:, attn:].reshape(TXT, heads, HEAD_DIM)
    length = lax.dynamic_index_in_dim(text_lengths, pick, 0, keepdims=False)
    live = jnp.arange(TXT, dtype=jnp.int32) < length
    text_query = jnp.dot(after_self, cross_query, preferred_element_type=jnp.float32)
    text_query = (head_norm(text_query, heads) * scale_q).astype(jnp.bfloat16)

    def cross_block(block):
        block_scores = jnp.einsum('phd,lhd->phl', block.astype(jnp.float32), text_key.astype(jnp.float32))
        block_weights = jnp.where(live, jnp.exp(block_scores), 0.0)
        block_total = lax.optimization_barrier(jnp.sum(block_weights, axis=-1))
        block_probs = lax.optimization_barrier(block_weights.astype(jnp.bfloat16)).astype(jnp.float32)
        block_mix = jnp.einsum('phl,lhd->phd', block_probs, text_value.astype(jnp.float32))
        return (block_mix / block_total[..., None]).astype(jnp.bfloat16)
    crossed = lax.map(cross_block, text_query.reshape(FRAMES, PIXELS, heads, HEAD_DIM)).reshape(-1, attn)
    cross_term = jnp.dot(crossed, cross_out, preferred_element_type=jnp.float32)
    frames_out = (after_self.astype(jnp.float32) + cross_term).astype(jnp.bfloat16)
    return frames_out.reshape(FRAMES, PIXELS, WIDTH)
```

```python
import functools
import math

import jax
import jax.numpy as jnp
from jax import lax
from jax.experimental import pallas as pl
from jax.experimental.pallas import tpu as pltpu
from jax.sharding import PartitionSpec as P

HEAD_DIM = 72


EPS = 1e-06


def spread_2(block, axis, owner):
    block = jnp.where(lax.axis_index(axis) == owner, block, jnp.zeros_like(block))
    return lax.psum(block, axis)


def layer_norm(values):
    mean = jnp.mean(values, axis=-1, keepdims=True)
    centred = values - mean
    spread = jnp.mean(centred * centred, axis=-1, keepdims=True)
    return centred * lax.rsqrt(spread + EPS)


def head_norm(values, heads):
    shaped = values.reshape(values.shape[:-1] + (heads, values.shape[-1] // heads))
    power = jnp.mean(shaped * shaped, axis=-1, keepdims=True)
    return shaped * lax.rsqrt(power + EPS)


def temporal_attention(qkv, heads, attn, scale_q):
    frames, patches = (qkv.shape[0], qkv.shape[1])
    query = (head_norm(qkv[..., :attn].astype(jnp.float32), heads) * scale_q).astype(jnp.bfloat16)
    key = head_norm(qkv[..., attn : 2 * attn].astype(jnp.float32), heads).astype(jnp.bfloat16)
    value = qkv[..., 2 * attn :].reshape(frames, patches, heads, attn // heads)
    scores = jnp.einsum("fphd,gphd->phfg", query, key, preferred_element_type=jnp.float32)
    weights = jnp.exp(scores)
    total = jnp.sum(weights, axis=-1)
    probs = weights.astype(jnp.bfloat16)
    mixed = jnp.einsum("phfg,gphd->fphd", probs, value, preferred_element_type=jnp.float32)
    attended = mixed / jnp.transpose(total, (2, 0, 1))[..., None]
    return attended.astype(jnp.bfloat16).reshape(frames, patches, attn)


def per_device(
    frames_in,
    modulation,
    self_proj,
    self_out,
    cross_query,
    cross_keyval,
    cross_out,
    text_bank,
    prompt_pick,
    text_lengths,
):
    count = lax.axis_size("seq")
    frame_rows, pixels, width = frames_in.shape
    attn = self_out.shape[0]
    heads = attn // HEAD_DIM
    scale_q = 1.0 / math.sqrt(HEAD_DIM)
    pix_dev = pixels // count
    frames = frame_rows * count
    tokens = frames_in.astype(jnp.float32)
    normed = (layer_norm(tokens) * (1.0 + modulation[1]) + modulation[0]).astype(jnp.bfloat16)
    switched = lax.all_to_all(normed, "seq", split_axis=1, concat_axis=0, tiled=True)
    flat_pix = switched.reshape(-1, width)
    qkv = jnp.dot(
        flat_pix,
        lax.all_gather(self_proj, "seq", axis=1, tiled=True),
        preferred_element_type=jnp.float32,
    ).astype(jnp.bfloat16)
    qkv = qkv.reshape(frames, pix_dev, 3 * attn)
    out_self, query_weight, out_cross = (
        lax.all_gather(self_out, "seq", axis=1, tiled=True),
        lax.all_gather(cross_query, "seq", axis=1, tiled=True),
        lax.all_gather(cross_out, "seq", axis=1, tiled=True),
    )
    attended = temporal_attention(qkv, heads, attn, scale_q)
    returned = lax.all_to_all(attended, "seq", split_axis=0, concat_axis=1, tiled=True)
    self_term = jnp.dot(returned.reshape(-1, attn), out_self, preferred_element_type=jnp.float32)
    after_self = (tokens.reshape(-1, width) + modulation[2] * self_term).astype(jnp.bfloat16)
    pick = prompt_pick[0]
    memory = spread_2(text_bank[0], "seq", pick)
    own_columns = jnp.dot(memory, cross_keyval, preferred_element_type=jnp.float32).astype(
        jnp.bfloat16
    )
    keyval = lax.all_gather(own_columns, "seq", axis=1, tiled=True)
    text_len = keyval.shape[0]
    text_key = head_norm(keyval[:, :attn].astype(jnp.float32), heads).astype(jnp.bfloat16)
    text_value = keyval[:, attn:].reshape(text_len, heads, HEAD_DIM)
    slots = jnp.arange(text_lengths.shape[0], dtype=jnp.int32)
    length = jnp.sum(jnp.where(slots == pick, text_lengths, 0))
    live = jnp.arange(text_len, dtype=jnp.int32) < length
    text_query = jnp.dot(after_self, query_weight, preferred_element_type=jnp.float32)
    text_query = (head_norm(text_query, heads) * scale_q).astype(jnp.bfloat16)
    cross_scores = jnp.einsum(
        "thd,lhd->thl", text_query, text_key, preferred_element_type=jnp.float32
    )
    cross_weights = jnp.where(live, jnp.exp(cross_scores), 0.0)
    cross_total = jnp.sum(cross_weights, axis=-1)
    cross_probs = cross_weights.astype(jnp.bfloat16)
    cross_mix = jnp.einsum(
        "thl,lhd->thd", cross_probs, text_value, preferred_element_type=jnp.float32
    )
    crossed = (cross_mix / cross_total[..., None]).astype(jnp.bfloat16).reshape(-1, attn)
    cross_term = jnp.dot(crossed, out_cross, preferred_element_type=jnp.float32)
    frames_out = (after_self.astype(jnp.float32) + cross_term).astype(jnp.bfloat16)
    return frames_out.reshape(frame_rows, pixels, width)


MESH = pl.DeviceIdType.MESH
CLIPS, LEVELS, CORES = 4, 4, 2


def greet(peers):
    barrier = pltpu.get_barrier_semaphore()
    for peer in peers:
        pl.semaphore_signal(barrier, inc=1, device_id=peer, device_id_type=MESH)
    pl.semaphore_wait(barrier, len(peers))


def places():
    clip, seq = lax.axis_index("clip"), lax.axis_index("seq")
    level, core = seq // CORES, seq % CORES
    sibling = level * CORES + (1 - core)
    levels = [lax.rem(level + step, LEVELS) for step in range(1, LEVELS)]
    clips = [lax.rem(clip + step, CLIPS) for step in range(1, CLIPS)]
    return clip, seq, level, core, sibling, levels, clips


def remote(src, dst, send_sem, recv_sem, clip, seq):
    return pltpu.make_async_remote_copy(
        src_ref=src,
        dst_ref=dst,
        send_sem=send_sem,
        recv_sem=recv_sem,
        device_id=(clip, seq),
        device_id_type=MESH,
    )


def gather_kernel(
    blocks_ref, pack_ref, memory_ref, tokens_ref, weights_ref, rows_ref,
    half_ref, slots_ref, held_ref,
    block_send, block_recv, pack_send, pack_recv, local_sem, half_sem, slice_send, slice_recv,
):
    clip, seq, level, core, sibling, levels, clips = places()
    peers = [lax.rem(seq + step, LEVELS * CORES) for step in range(1, LEVELS * CORES)]
    greet([(clip, peer) for peer in peers] + [(other, seq) for other in clips])
    piece = pack_ref.shape[0] // CLIPS
    pieces = [clip] + clips

    def rows(index):
        return pl.ds(pl.multiple_of(index * piece, 16), piece)

    own_rows = [pltpu.make_async_copy(pack_ref, weights_ref.at[seq], local_sem.at[0]),
                pltpu.make_async_copy(blocks_ref.at[seq], tokens_ref.at[seq], local_sem.at[1])]
    for copy in own_rows:
        copy.start()
    half = held_ref.shape[0]
    swap = remote(
        memory_ref.at[pl.ds(pl.multiple_of((1 - core) * half, 16), half)], half_ref,
        half_sem.at[0], half_sem.at[1], clip, sibling,
    )
    swap.start()
    sends = [swap]

    def weight(src, shard, part, index, to_clip, to_seq):
        copy = remote(
            src, weights_ref.at[shard, rows(part)], pack_send.at[index],
            pack_recv.at[shard, part], to_clip, to_seq,
        )
        copy.start()
        sends.append(copy)

    def arrived(shard, part):
        view = weights_ref.at[shard, rows(part)]
        pltpu.make_async_copy(view, view, pack_recv.at[shard, part]).wait()

    for n, other in enumerate(levels):
        weight(pack_ref.at[rows(clip)], seq, clip, n, clip, other * CORES + core)
    for n, peer in enumerate(peers):
        copy = remote(
            blocks_ref.at[peer], tokens_ref.at[seq], block_send.at[n], block_recv.at[seq], clip, peer
        )
        copy.start()
        sends.append(copy)
    for n, part in enumerate(pieces):
        weight(pack_ref.at[rows(part)], seq, part, 3 + n, clip, sibling)

    swap.wait_recv()
    held_ref[...] = memory_ref[pl.ds(pl.multiple_of(core * half, 16), half)] + half_ref[...]
    size = half // LEVELS
    slices = []
    for n, other in enumerate(levels):
        copy = remote(
            held_ref.at[pl.ds(pl.multiple_of(other * size, 16), size)], slots_ref.at[level],
            slice_send.at[n], slice_recv.at[level], clip, other * CORES + core,
        )
        copy.start()
        sends.append(copy)

    index = 7
    for other in levels:
        shard = other * CORES + core
        arrived(shard, clip)
        for to in clips:
            weight(weights_ref.at[shard, rows(clip)], shard, clip, index, to, seq)
            index += 1
        weight(weights_ref.at[shard, rows(clip)], shard, clip, index, clip, sibling)
        index += 1
    for other in levels:
        shard = other * CORES + core
        for part in clips:
            arrived(shard, part)
            weight(weights_ref.at[shard, rows(part)], shard, part, index, clip, sibling)
            index += 1

    total = held_ref[pl.ds(pl.multiple_of(level * size, 16), size)]
    for other in levels:
        pltpu.make_async_copy(slots_ref.at[other], slots_ref.at[other], slice_recv.at[other]).wait()
        total = total + slots_ref[other]
    rows_ref[...] = total
    for other in [level] + levels:
        for part in pieces:
            arrived(other * CORES + 1 - core, part)
    for peer in peers:
        view = tokens_ref.at[peer]
        pltpu.make_async_copy(view, view, block_recv.at[peer]).wait()
    for copy in own_rows:
        copy.wait()
    for copy in sends:
        copy.wait_send()


def gather(blocks, pack, memory):
    count, rows, width = blocks.shape
    text, dma = memory.shape[0], pltpu.SemaphoreType.DMA
    anywhere = pl.BlockSpec(memory_space=pl.ANY)
    vmem = pl.BlockSpec(memory_space=pltpu.VMEM)
    size = text // count
    return pl.pallas_call(
        gather_kernel,
        out_shape=(
            jax.ShapeDtypeStruct(blocks.shape, blocks.dtype),
            jax.ShapeDtypeStruct((count,) + pack.shape, pack.dtype),
            jax.ShapeDtypeStruct((size, width), memory.dtype),
        ),
        in_specs=[anywhere, anywhere, vmem],
        out_specs=(anywhere, anywhere, vmem),
        scratch_shapes=[
            pltpu.VMEM((text // CORES, width), memory.dtype),
            pltpu.VMEM((LEVELS, size, width), memory.dtype),
            pltpu.VMEM((text // CORES, width), memory.dtype),
            dma((count - 1,)),
            dma((count,)),
            dma((28,)),
            dma((count, CLIPS)),
            dma((2,)),
            dma((2,)),
            dma((LEVELS - 1,)),
            dma((LEVELS,)),
        ],
        compiler_params=pltpu.CompilerParams(collective_id=0, has_side_effects=True),
    )(blocks, pack, memory)


def return_kernel(blocks_ref, text_ref, tokens_ref, keyval_ref,
                  block_send, block_recv, text_send, text_recv, local_sem):
    clip, seq, level, core, sibling, levels, _ = places()
    peers = [lax.rem(seq + step, LEVELS * CORES) for step in range(1, LEVELS * CORES)]
    greet([(clip, peer) for peer in peers])
    own = [pltpu.make_async_copy(text_ref, keyval_ref.at[seq], local_sem.at[0]),
           pltpu.make_async_copy(blocks_ref.at[seq], tokens_ref.at[seq], local_sem.at[1])]
    for copy in own:
        copy.start()
    sends = []

    def text(src, shard, index, to):
        copy = remote(src, keyval_ref.at[shard], text_send.at[index], text_recv.at[shard], clip, to)
        copy.start()
        sends.append(copy)

    def arrived(ref, sem, shard):
        pltpu.make_async_copy(ref.at[shard], ref.at[shard], sem.at[shard]).wait()

    for n, other in enumerate(levels):
        text(text_ref, seq, n, other * CORES + core)
    for n, peer in enumerate(peers):
        copy = remote(
            blocks_ref.at[peer], tokens_ref.at[seq], block_send.at[n], block_recv.at[seq], clip, peer
        )
        copy.start()
        sends.append(copy)
    text(text_ref, seq, 3, sibling)
    for n, other in enumerate(levels):
        shard = other * CORES + core
        arrived(keyval_ref, text_recv, shard)
        text(keyval_ref.at[shard], shard, 4 + n, sibling)
    for other in [level] + levels:
        arrived(keyval_ref, text_recv, other * CORES + 1 - core)
    for peer in peers:
        arrived(tokens_ref, block_recv, peer)
    for copy in own:
        copy.wait()
    for copy in sends:
        copy.wait_send()


def give_back(blocks, text):
    count, dma = blocks.shape[0], pltpu.SemaphoreType.DMA
    anywhere = pl.BlockSpec(memory_space=pl.ANY)
    return pl.pallas_call(
        return_kernel,
        out_shape=(
            jax.ShapeDtypeStruct(blocks.shape, blocks.dtype),
            jax.ShapeDtypeStruct((count,) + text.shape, text.dtype),
        ),
        in_specs=[anywhere, anywhere],
        out_specs=(anywhere, anywhere),
        scratch_shapes=[dma((count - 1,)), dma((count,)), dma((7,)), dma((count,)), dma((2,))],
        compiler_params=pltpu.CompilerParams(collective_id=1, has_side_effects=True),
    )(blocks, text)


def nt(left, right):
    return lax.dot_general(
        left, right, (((1,), (1,)), ((), ())), preferred_element_type=jnp.float32
    )


def per_device_shared(
    frames_in,
    modulation,
    self_proj,
    self_out,
    cross_query,
    cross_keyval,
    cross_out,
    text_bank,
    prompt_pick,
    text_lengths,
):
    count = lax.axis_size("seq")
    frame_rows, pixels, width = frames_in.shape
    attn = self_out.shape[0]
    heads = attn // HEAD_DIM
    scale_q = 1.0 / math.sqrt(HEAD_DIM)
    pix_dev = pixels // count
    frames = frame_rows * count
    block = frame_rows * pix_dev
    pick = prompt_pick[0]
    memory = text_bank[0]
    memory = jnp.where(lax.axis_index("seq") == pick, memory, jnp.zeros_like(memory))
    tokens = frames_in.astype(jnp.float32)
    normed = (layer_norm(tokens) * (1.0 + modulation[1]) + modulation[0]).astype(jnp.bfloat16)
    blocks = normed.reshape(frame_rows, count, pix_dev, width).transpose(1, 0, 2, 3)
    blocks = blocks.reshape(count, block, width)
    pack = jnp.concatenate(
        [
            self_proj.T,
            cross_query.T,
            cross_keyval.T,
            jnp.concatenate([self_out.T, cross_out.T], axis=1),
        ],
        axis=0,
    )
    ends = [0]
    for part in (self_proj, cross_query, cross_keyval, self_out):
        ends.append(ends[-1] + part.shape[1])
    switched, weights, text_rows = gather(blocks, pack, memory)

    def full(index):
        return weights[:, ends[index] : ends[index + 1]].reshape(-1, width)

    proj, query_weight, text_weight, outs = full(0), full(1), full(2), full(3)
    qkv = nt(switched.reshape(-1, width), proj).astype(jnp.bfloat16)
    qkv = qkv.reshape(frames, pix_dev, 3 * attn)
    own_keyval = nt(text_rows, text_weight).astype(jnp.bfloat16)
    attended = temporal_attention(qkv, heads, attn, scale_q)
    returned, keyval = give_back(attended.reshape(count, block, attn), own_keyval)
    returned = returned.reshape(count, frame_rows, pix_dev, attn).transpose(1, 0, 2, 3)
    self_term = nt(returned.reshape(-1, attn), outs[:, :attn])
    after_self = (tokens.reshape(-1, width) + modulation[2] * self_term).astype(jnp.bfloat16)
    text_len = count * text_rows.shape[0]
    keyval = keyval.reshape(LEVELS, CORES, -1, 2 * attn).transpose(1, 0, 2, 3)
    keyval = keyval.reshape(text_len, 2 * attn)
    text_key = head_norm(keyval[:, :attn].astype(jnp.float32), heads).astype(jnp.bfloat16)
    text_value = keyval[:, attn:].reshape(text_len, heads, HEAD_DIM)
    slots = jnp.arange(text_lengths.shape[0], dtype=jnp.int32)
    length = jnp.sum(jnp.where(slots == pick, text_lengths, 0))
    live = jnp.arange(text_len, dtype=jnp.int32) < length
    text_query = nt(after_self, query_weight)
    text_query = (head_norm(text_query, heads) * scale_q).astype(jnp.bfloat16)
    cross_scores = jnp.einsum(
        "thd,lhd->thl", text_query, text_key, preferred_element_type=jnp.float32
    )
    cross_weights = jnp.where(live, jnp.exp(cross_scores), 0.0)
    cross_total = jnp.sum(cross_weights, axis=-1)
    cross_probs = cross_weights.astype(jnp.bfloat16)
    cross_mix = jnp.einsum(
        "thl,lhd->thd", cross_probs, text_value, preferred_element_type=jnp.float32
    )
    crossed = (cross_mix / cross_total[..., None]).astype(jnp.bfloat16).reshape(-1, attn)
    cross_term = nt(crossed, outs[:, attn:])
    frames_out = (after_self.astype(jnp.float32) + cross_term).astype(jnp.bfloat16)
    return frames_out.reshape(frame_rows, pixels, width)


def solution(mesh):
    shared = mesh.shape["clip"] == CLIPS and mesh.shape["seq"] == LEVELS * CORES
    placed = (
        P(("clip", "seq"), None, None),
        P("clip", None),
        P(None, "seq"),
        P(None, "seq"),
        P(None, "seq"),
        P(None, "seq"),
        P(None, "seq"),
        P("seq", None, None),
        P("clip"),
        P(),
    )
    return jax.shard_map(
        per_device_shared if shared else per_device,
        mesh=mesh,
        in_specs=placed,
        out_specs=P(("clip", "seq"), None, None),
        check_vma=False,
    )
```

```python
import functools
import math

import jax
import jax.numpy as jnp
from jax import lax
from jax.experimental import pallas as pl
from jax.experimental.pallas import tpu as pltpu
from jax.sharding import PartitionSpec as P

HEAD_DIM = 72


EPS = 1e-06


def spread_2(block, axis, owner):
    block = jnp.where(lax.axis_index(axis) == owner, block, jnp.zeros_like(block))
    return lax.psum(block, axis)


def layer_norm(values):
    mean = jnp.mean(values, axis=-1, keepdims=True)
    centred = values - mean
    spread = jnp.mean(centred * centred, axis=-1, keepdims=True)
    return centred * lax.rsqrt(spread + EPS)


def head_norm(values, heads):
    shaped = values.reshape(values.shape[:-1] + (heads, values.shape[-1] // heads))
    power = jnp.mean(shaped * shaped, axis=-1, keepdims=True)
    return shaped * lax.rsqrt(power + EPS)


def temporal_attention(qkv, heads, attn, scale_q):
    frames, patches = (qkv.shape[0], qkv.shape[1])
    query = (head_norm(qkv[..., :attn].astype(jnp.float32), heads) * scale_q).astype(jnp.bfloat16)
    key = head_norm(qkv[..., attn : 2 * attn].astype(jnp.float32), heads).astype(jnp.bfloat16)
    value = qkv[..., 2 * attn :].reshape(frames, patches, heads, attn // heads)
    scores = jnp.einsum("fphd,gphd->phfg", query, key, preferred_element_type=jnp.float32)
    weights = jnp.exp(scores)
    total = jnp.sum(weights, axis=-1)
    probs = weights.astype(jnp.bfloat16)
    mixed = jnp.einsum("phfg,gphd->fphd", probs, value, preferred_element_type=jnp.float32)
    attended = mixed / jnp.transpose(total, (2, 0, 1))[..., None]
    return attended.astype(jnp.bfloat16).reshape(frames, patches, attn)


def per_device(
    frames_in,
    modulation,
    self_proj,
    self_out,
    cross_query,
    cross_keyval,
    cross_out,
    text_bank,
    prompt_pick,
    text_lengths,
):
    count = lax.axis_size("seq")
    frame_rows, pixels, width = frames_in.shape
    attn = self_out.shape[0]
    heads = attn // HEAD_DIM
    scale_q = 1.0 / math.sqrt(HEAD_DIM)
    pix_dev = pixels // count
    frames = frame_rows * count
    tokens = frames_in.astype(jnp.float32)
    normed = (layer_norm(tokens) * (1.0 + modulation[1]) + modulation[0]).astype(jnp.bfloat16)
    switched = lax.all_to_all(normed, "seq", split_axis=1, concat_axis=0, tiled=True)
    flat_pix = switched.reshape(-1, width)
    qkv = jnp.dot(
        flat_pix,
        lax.all_gather(self_proj, "seq", axis=1, tiled=True),
        preferred_element_type=jnp.float32,
    ).astype(jnp.bfloat16)
    qkv = qkv.reshape(frames, pix_dev, 3 * attn)
    out_self, query_weight, out_cross = (
        lax.all_gather(self_out, "seq", axis=1, tiled=True),
        lax.all_gather(cross_query, "seq", axis=1, tiled=True),
        lax.all_gather(cross_out, "seq", axis=1, tiled=True),
    )
    attended = temporal_attention(qkv, heads, attn, scale_q)
    returned = lax.all_to_all(attended, "seq", split_axis=0, concat_axis=1, tiled=True)
    self_term = jnp.dot(returned.reshape(-1, attn), out_self, preferred_element_type=jnp.float32)
    after_self = (tokens.reshape(-1, width) + modulation[2] * self_term).astype(jnp.bfloat16)
    pick = prompt_pick[0]
    memory = spread_2(text_bank[0], "seq", pick)
    own_columns = jnp.dot(memory, cross_keyval, preferred_element_type=jnp.float32).astype(
        jnp.bfloat16
    )
    keyval = lax.all_gather(own_columns, "seq", axis=1, tiled=True)
    text_len = keyval.shape[0]
    text_key = head_norm(keyval[:, :attn].astype(jnp.float32), heads).astype(jnp.bfloat16)
    text_value = keyval[:, attn:].reshape(text_len, heads, HEAD_DIM)
    slots = jnp.arange(text_lengths.shape[0], dtype=jnp.int32)
    length = jnp.sum(jnp.where(slots == pick, text_lengths, 0))
    live = jnp.arange(text_len, dtype=jnp.int32) < length
    text_query = jnp.dot(after_self, query_weight, preferred_element_type=jnp.float32)
    text_query = (head_norm(text_query, heads) * scale_q).astype(jnp.bfloat16)
    cross_scores = jnp.einsum(
        "thd,lhd->thl", text_query, text_key, preferred_element_type=jnp.float32
    )
    cross_weights = jnp.where(live, jnp.exp(cross_scores), 0.0)
    cross_total = jnp.sum(cross_weights, axis=-1)
    cross_probs = cross_weights.astype(jnp.bfloat16)
    cross_mix = jnp.einsum(
        "thl,lhd->thd", cross_probs, text_value, preferred_element_type=jnp.float32
    )
    crossed = (cross_mix / cross_total[..., None]).astype(jnp.bfloat16).reshape(-1, attn)
    cross_term = jnp.dot(crossed, out_cross, preferred_element_type=jnp.float32)
    frames_out = (after_self.astype(jnp.float32) + cross_term).astype(jnp.bfloat16)
    return frames_out.reshape(frame_rows, pixels, width)


MESH = pl.DeviceIdType.MESH
CLIPS, LEVELS, CORES = 4, 4, 2


def greet(peers):
    barrier = pltpu.get_barrier_semaphore()
    for peer in peers:
        pl.semaphore_signal(barrier, inc=1, device_id=peer, device_id_type=MESH)
    pl.semaphore_wait(barrier, len(peers))


def places():
    clip, seq = lax.axis_index("clip"), lax.axis_index("seq")
    level, core = seq // CORES, seq % CORES
    sibling = level * CORES + (1 - core)
    levels = [lax.rem(level + step, LEVELS) for step in range(1, LEVELS)]
    clips = [lax.rem(clip + step, CLIPS) for step in range(1, CLIPS)]
    return clip, seq, level, core, sibling, levels, clips


def remote(src, dst, send_sem, recv_sem, clip, seq):
    return pltpu.make_async_remote_copy(
        src_ref=src,
        dst_ref=dst,
        send_sem=send_sem,
        recv_sem=recv_sem,
        device_id=(clip, seq),
        device_id_type=MESH,
    )


SUBS = ((0, 64), (64, 48))
OUT_ROWS, QUERY_ROWS, PROJ_ROWS = 144, 80, 224
PACKED = OUT_ROWS + QUERY_ROWS + PROJ_ROWS
GRANT = 56 * 1024 * 1024


def gather_kernel(
    frames_ref, modulation_ref, pack_ref, memory_ref, mask_ref,
    tokens_ref, weights_ref, text_ref,
    normed_ref, blocks_ref, masked_ref, half_ref, held_ref, slots_ref, own_ref,
    block_send, block_recv, pack_send, pack_recv, local_sem, half_sem,
    slice_send, slice_recv, text_send, text_recv,
):
    clip, seq, level, core, sibling, levels, clips = places()
    peers = [lax.rem(seq + step, LEVELS * CORES) for step in range(1, LEVELS * CORES)]
    greet([(clip, peer) for peer in peers] + [(other, seq) for other in clips])
    piece = pack_ref.shape[0] // CLIPS
    pieces = [clip] + clips
    sends = []

    def rows(part, sub):
        start, size = SUBS[sub]
        return pl.ds(pl.multiple_of(part * piece + start, 16), size)

    def start(copy):
        copy.start()
        sends.append(copy)

    def weight(src, shard, part, sub, index, to_clip, to_seq):
        start(remote(
            src.at[rows(part, sub)], weights_ref.at[shard, rows(part, sub)],
            pack_send.at[sub, index], pack_recv.at[sub, shard, part], to_clip, to_seq,
        ))

    def arrived(shard, part, sub):
        view = weights_ref.at[shard, rows(part, sub)]
        pltpu.make_async_copy(view, view, pack_recv.at[sub, shard, part]).wait()

    for sub in range(2):
        for n, other in enumerate(levels):
            weight(pack_ref, seq, clip, sub, n, clip, other * CORES + core)
    local = [pltpu.make_async_copy(pack_ref, weights_ref.at[seq], local_sem.at[0])]
    local[0].start()

    masked_ref[...] = memory_ref[...] * mask_ref[...]
    half = held_ref.shape[0]
    swap = remote(
        masked_ref.at[pl.ds(pl.multiple_of((1 - core) * half, 16), half)], half_ref,
        half_sem.at[0], half_sem.at[1], clip, sibling,
    )
    start(swap)
    for sub in range(2):
        for n, part in enumerate(pieces):
            weight(pack_ref, seq, part, sub, 3 + n, clip, sibling)

    frame_rows, pixels, width = frames_ref.shape
    gain, shift = 1.0 + modulation_ref[1:2], modulation_ref[0:1]
    for frame in range(frame_rows):
        normed_ref[frame] = layer_norm(frames_ref[frame].astype(jnp.float32)) * gain + shift
    count = blocks_ref.shape[0]
    pix = pixels // count
    for to in range(count):
        block = normed_ref[:, to * pix : (to + 1) * pix].reshape(frame_rows * pix, width)
        blocks_ref[to] = block.astype(jnp.bfloat16)
    local.append(pltpu.make_async_copy(blocks_ref.at[seq], tokens_ref.at[seq], local_sem.at[1]))
    local[1].start()
    for n, peer in enumerate(peers):
        start(remote(
            blocks_ref.at[peer], tokens_ref.at[seq], block_send.at[n], block_recv.at[seq], clip, peer
        ))

    swap.wait_recv()
    held_ref[...] = masked_ref[pl.ds(pl.multiple_of(core * half, 16), half)] + half_ref[...]
    size = half // LEVELS
    for n, other in enumerate(levels):
        start(remote(
            held_ref.at[pl.ds(pl.multiple_of(other * size, 16), size)], slots_ref.at[level],
            slice_send.at[n], slice_recv.at[level], clip, other * CORES + core,
        ))

    def forward(sub):
        index = 7
        for other in levels:
            shard = other * CORES + core
            arrived(shard, clip, sub)
            for to in clips:
                weight(weights_ref.at[shard], shard, clip, sub, index, to, seq)
                index += 1
            weight(weights_ref.at[shard], shard, clip, sub, index, clip, sibling)
            index += 1

    def across(sub):
        index = 19
        for other in levels:
            shard = other * CORES + core
            for part in clips:
                arrived(shard, part, sub)
                weight(weights_ref.at[shard], shard, part, sub, index, clip, sibling)
                index += 1

    def text(src, place, index, to):
        start(remote(src, text_ref.at[place], text_send.at[index], text_recv.at[place], clip, to))

    def wait(ref, sem, place):
        pltpu.make_async_copy(ref.at[place], ref.at[place], sem.at[place]).wait()

    forward(0)
    total = held_ref[pl.ds(pl.multiple_of(level * size, 16), size)]
    for other in levels:
        wait(slots_ref, slice_recv, other)
        total = total + slots_ref[other]
    own_ref[...] = total
    place = core * LEVELS + level
    local.append(pltpu.make_async_copy(own_ref, text_ref.at[place], local_sem.at[2]))
    local[2].start()
    for n, other in enumerate(levels):
        text(own_ref, place, n, other * CORES + core)
    text(own_ref, place, 3, sibling)
    forward(1)
    for n, other in enumerate(levels):
        wait(text_ref, text_recv, core * LEVELS + other)
        text(text_ref.at[core * LEVELS + other], core * LEVELS + other, 4 + n, sibling)
    for sub in range(2):
        across(sub)
    for other in [level] + levels:
        for part in pieces:
            for sub in range(2):
                arrived(other * CORES + 1 - core, part, sub)
        wait(text_ref, text_recv, (1 - core) * LEVELS + other)
    for peer in peers:
        wait(tokens_ref, block_recv, peer)
    for copy in local:
        copy.wait()
    for copy in sends:
        copy.wait_send()


def gather(frames_in, modulation, pack, memory, mask):
    frame_rows, pixels, width = frames_in.shape
    count, kind, text = LEVELS * CORES, frames_in.dtype, memory.shape[0]
    dma = pltpu.SemaphoreType.DMA
    anywhere = pl.BlockSpec(memory_space=pl.ANY)
    vmem = pl.BlockSpec(memory_space=pltpu.VMEM)
    block, size = frame_rows * pixels // count, text // count
    return pl.pallas_call(
        gather_kernel,
        out_shape=(
            jax.ShapeDtypeStruct((count, block, width), kind),
            jax.ShapeDtypeStruct((count,) + pack.shape, kind),
            jax.ShapeDtypeStruct((count, size, width), kind),
        ),
        in_specs=[vmem, vmem, anywhere, vmem, vmem],
        out_specs=(anywhere,) * 3,
        scratch_shapes=[
            pltpu.VMEM((frame_rows, pixels, width), jnp.float32),
            pltpu.VMEM((count, block, width), kind),
            pltpu.VMEM((text, width), kind),
            pltpu.VMEM((text // CORES, width), kind),
            pltpu.VMEM((text // CORES, width), kind),
            pltpu.VMEM((LEVELS, size, width), kind),
            pltpu.VMEM((size, width), kind),
            dma((count - 1,)),
            dma((count,)),
            dma((2, 28)),
            dma((2, count, CLIPS)),
            dma((3,)),
            dma((2,)),
            dma((LEVELS - 1,)),
            dma((LEVELS,)),
            dma((7,)),
            dma((count,)),
        ],
        compiler_params=pltpu.CompilerParams(
            collective_id=0, has_side_effects=True, vmem_limit_bytes=GRANT
        ),
    )(frames_in, modulation, pack, memory, mask)


def return_kernel(blocks_ref, text_ref, tokens_ref, keyval_ref,
                  block_send, block_recv, text_send, text_recv, local_sem):
    clip, seq, level, core, sibling, levels, _ = places()
    peers = [lax.rem(seq + step, LEVELS * CORES) for step in range(1, LEVELS * CORES)]
    greet([(clip, peer) for peer in peers])
    own = [pltpu.make_async_copy(text_ref, keyval_ref.at[seq], local_sem.at[0]),
           pltpu.make_async_copy(blocks_ref.at[seq], tokens_ref.at[seq], local_sem.at[1])]
    for copy in own:
        copy.start()
    sends = []

    def text(src, shard, index, to):
        copy = remote(src, keyval_ref.at[shard], text_send.at[index], text_recv.at[shard], clip, to)
        copy.start()
        sends.append(copy)

    def arrived(ref, sem, shard):
        pltpu.make_async_copy(ref.at[shard], ref.at[shard], sem.at[shard]).wait()

    for n, other in enumerate(levels):
        text(text_ref, seq, n, other * CORES + core)
    for n, peer in enumerate(peers):
        copy = remote(
            blocks_ref.at[peer], tokens_ref.at[seq], block_send.at[n], block_recv.at[seq], clip, peer
        )
        copy.start()
        sends.append(copy)
    text(text_ref, seq, 3, sibling)
    for n, other in enumerate(levels):
        shard = other * CORES + core
        arrived(keyval_ref, text_recv, shard)
        text(keyval_ref.at[shard], shard, 4 + n, sibling)
    for other in [level] + levels:
        arrived(keyval_ref, text_recv, other * CORES + 1 - core)
    for peer in peers:
        arrived(tokens_ref, block_recv, peer)
    for copy in own:
        copy.wait()
    for copy in sends:
        copy.wait_send()


def give_back(blocks, text):
    count, dma = blocks.shape[0], pltpu.SemaphoreType.DMA
    anywhere = pl.BlockSpec(memory_space=pl.ANY)
    return pl.pallas_call(
        return_kernel,
        out_shape=(
            jax.ShapeDtypeStruct(blocks.shape, blocks.dtype),
            jax.ShapeDtypeStruct((count,) + text.shape, text.dtype),
        ),
        in_specs=[anywhere, anywhere],
        out_specs=(anywhere, anywhere),
        scratch_shapes=[dma((count - 1,)), dma((count,)), dma((7,)), dma((count,)), dma((2,))],
        compiler_params=pltpu.CompilerParams(collective_id=1, has_side_effects=True),
    )(blocks, text)


def nt(left, right):
    return lax.dot_general(
        left, right, (((1,), (1,)), ((), ())), preferred_element_type=jnp.float32
    )


def unit(values, axis):
    power = jnp.sum(values * values, axis=axis, keepdims=True) * (1.0 / HEAD_DIM)
    return values * lax.rsqrt(power + EPS)


def self_kernel(pix, tokens_ref, weights_ref, text_ref, keyval_ref, out_ref, text_out_ref, qkv_ref):
    tokens = tokens_ref[...]
    count = weights_ref.shape[0]
    per = 3
    heads = count * per // 3
    for shard in range(count):
        columns = nt(tokens, weights_ref[shard, OUT_ROWS + QUERY_ROWS :])
        for j in range(per):
            part = columns[:, j * HEAD_DIM : (j + 1) * HEAD_DIM]
            qkv_ref[shard * per + j] = part.astype(jnp.bfloat16)
    text_out_ref[...] = nt(keyval_ref[...], text_ref[...]).astype(jnp.bfloat16)
    rows = tokens.shape[0]
    row = lax.broadcasted_iota(jnp.int32, (rows, rows), 0)
    column = lax.broadcasted_iota(jnp.int32, (rows, rows), 1)
    same = (row % pix) == (column % pix)
    scale_q = 1.0 / math.sqrt(HEAD_DIM)
    outs = []
    for head in range(heads):
        query = (unit(qkv_ref[head].astype(jnp.float32), 1) * scale_q).astype(jnp.bfloat16)
        key = unit(qkv_ref[heads + head].astype(jnp.float32), 1).astype(jnp.bfloat16)
        weights = jnp.where(same, jnp.exp(nt(query, key)), 0.0)
        total = jnp.sum(weights, axis=1, keepdims=True)
        mixed = jnp.dot(
            weights.astype(jnp.bfloat16), qkv_ref[2 * heads + head],
            preferred_element_type=jnp.float32,
        )
        outs.append(mixed / total)
    pad = out_ref.shape[1] - heads * HEAD_DIM
    outs.append(jnp.zeros((rows, pad), jnp.float32))
    out_ref[...] = jnp.concatenate(outs, axis=1).astype(jnp.bfloat16)


def cross_kernel(
    returned_ref, frames_ref, modulation_ref, weights_ref, keyval_ref, live_ref, out_ref,
    attended_ref, out_weight_ref,
):
    count, block, lanes = returned_ref.shape
    frame_rows, pixels, width = frames_ref.shape
    pix = block // frame_rows
    for src in range(count):
        part = returned_ref[src].astype(jnp.float32)
        for frame in range(frame_rows):
            at = frame * pixels + src * pix
            attended_ref[at : at + pix] = part[frame * pix : (frame + 1) * pix]
        out_weight_ref[src * OUT_ROWS : (src + 1) * OUT_ROWS] = weights_ref[src, :OUT_ROWS]
    self_term = nt(attended_ref[...].astype(jnp.bfloat16), out_weight_ref[:, :lanes])
    tokens = frames_ref[...].astype(jnp.float32).reshape(frame_rows * pixels, width)
    after_self = (tokens + modulation_ref[2:3] * self_term).astype(jnp.bfloat16)
    live = live_ref[...] > 0.0
    heads = count
    scale_q = 1.0 / math.sqrt(HEAD_DIM)
    outs = [jnp.zeros((tokens.shape[0], lanes - heads * HEAD_DIM), jnp.float32)]
    per = keyval_ref.shape[1] // HEAD_DIM

    def of_head(index):
        shard = keyval_ref[index // per].astype(jnp.float32)
        return shard[(index % per) * HEAD_DIM : (index % per + 1) * HEAD_DIM]

    for head in range(heads):
        query = nt(after_self, weights_ref[head, OUT_ROWS : OUT_ROWS + QUERY_ROWS])
        query = (unit(query, 1) * scale_q).astype(jnp.bfloat16)[:, :HEAD_DIM]
        key = unit(of_head(head), 0).astype(jnp.bfloat16)
        scores = jnp.dot(query, key, preferred_element_type=jnp.float32)
        weights = jnp.where(live, jnp.exp(scores), 0.0)
        total = jnp.sum(weights, axis=1, keepdims=True)
        value = of_head(heads + head).astype(jnp.bfloat16)
        outs.append(nt(weights.astype(jnp.bfloat16), value) / total)
    crossed = jnp.concatenate(outs, axis=1).astype(jnp.bfloat16)
    cross_term = nt(crossed, out_weight_ref[:, width - lanes :])
    result = (after_self.astype(jnp.float32) + cross_term).astype(jnp.bfloat16)
    out_ref[...] = result.reshape(frame_rows, pixels, width)


def per_device_shared(
    frames_in,
    modulation,
    self_proj,
    self_out,
    cross_query,
    cross_keyval,
    cross_out,
    text_bank,
    prompt_pick,
    text_lengths,
):
    count = lax.axis_size("seq")
    frame_rows, pixels, width = frames_in.shape
    attn = self_out.shape[0]
    block = frame_rows * pixels // count
    lanes = -(-attn // 128) * 128
    pick = prompt_pick[0]
    memory = text_bank[0]
    text_len = memory.shape[0]
    mine = (lax.axis_index("seq") == pick).astype(jnp.bfloat16)
    mask = jnp.full((1, width), mine)

    def fill(part, rows):
        return jnp.pad(part, ((0, rows - part.shape[0]), (0, 0)))

    pack = jnp.concatenate(
        [
            jnp.concatenate([self_out.T, cross_out.T], axis=1),
            fill(cross_query.T, QUERY_ROWS),
            fill(self_proj.T, PROJ_ROWS),
        ],
        axis=0,
    )
    switched, weights, text = gather(frames_in, modulation, pack, memory, mask)
    attended, own_keyval = pl.pallas_call(
        functools.partial(self_kernel, pixels // count),
        out_shape=(
            jax.ShapeDtypeStruct((count * block, lanes), jnp.bfloat16),
            jax.ShapeDtypeStruct((cross_keyval.shape[1], text_len), jnp.bfloat16),
        ),
        scratch_shapes=[pltpu.VMEM((3 * attn // HEAD_DIM, count * block, HEAD_DIM), jnp.bfloat16)],
        compiler_params=pltpu.CompilerParams(vmem_limit_bytes=GRANT),
    )(switched.reshape(-1, width), weights, text.reshape(text_len, width), cross_keyval.T)
    returned, keyval = give_back(attended.reshape(count, block, lanes), own_keyval)
    slots = jnp.arange(text_lengths.shape[0], dtype=jnp.int32)
    length = jnp.sum(jnp.where(slots == pick, text_lengths, 0))
    live = (jnp.arange(text_len, dtype=jnp.int32) < length).astype(jnp.float32)[None]
    return pl.pallas_call(
        cross_kernel,
        out_shape=jax.ShapeDtypeStruct(frames_in.shape, jnp.bfloat16),
        scratch_shapes=[
            pltpu.VMEM((frame_rows * pixels, lanes), jnp.float32),
            pltpu.VMEM((count * OUT_ROWS, width), jnp.bfloat16),
        ],
        compiler_params=pltpu.CompilerParams(vmem_limit_bytes=GRANT),
    )(returned, frames_in, modulation, weights, keyval, live)


def solution(mesh):
    shared = mesh.shape["clip"] == CLIPS and mesh.shape["seq"] == LEVELS * CORES
    placed = (
        P(("clip", "seq"), None, None),
        P("clip", None),
        P(None, "seq"),
        P(None, "seq"),
        P(None, "seq"),
        P(None, "seq"),
        P(None, "seq"),
        P("seq", None, None),
        P("clip"),
        P(),
    )
    return jax.shard_map(
        per_device_shared if shared else per_device,
        mesh=mesh,
        in_specs=placed,
        out_specs=P(("clip", "seq"), None, None),
        check_vma=False,
    )
```

```python
import functools
import math

import jax
import jax.numpy as jnp
from jax import lax
from jax.experimental import pallas as pl
from jax.experimental.pallas import tpu as pltpu
from jax.sharding import PartitionSpec as P

HEAD_DIM = 72


EPS = 1e-06


def spread_2(block, axis, owner):
    block = jnp.where(lax.axis_index(axis) == owner, block, jnp.zeros_like(block))
    return lax.psum(block, axis)


def layer_norm(values):
    mean = jnp.mean(values, axis=-1, keepdims=True)
    centred = values - mean
    spread = jnp.mean(centred * centred, axis=-1, keepdims=True)
    return centred * lax.rsqrt(spread + EPS)


def head_norm(values, heads):
    shaped = values.reshape(values.shape[:-1] + (heads, values.shape[-1] // heads))
    power = jnp.mean(shaped * shaped, axis=-1, keepdims=True)
    return shaped * lax.rsqrt(power + EPS)


def temporal_attention(qkv, heads, attn, scale_q):
    frames, patches = (qkv.shape[0], qkv.shape[1])
    query = (head_norm(qkv[..., :attn].astype(jnp.float32), heads) * scale_q).astype(jnp.bfloat16)
    key = head_norm(qkv[..., attn : 2 * attn].astype(jnp.float32), heads).astype(jnp.bfloat16)
    value = qkv[..., 2 * attn :].reshape(frames, patches, heads, attn // heads)
    scores = jnp.einsum("fphd,gphd->phfg", query, key, preferred_element_type=jnp.float32)
    weights = jnp.exp(scores)
    total = jnp.sum(weights, axis=-1)
    probs = weights.astype(jnp.bfloat16)
    mixed = jnp.einsum("phfg,gphd->fphd", probs, value, preferred_element_type=jnp.float32)
    attended = mixed / jnp.transpose(total, (2, 0, 1))[..., None]
    return attended.astype(jnp.bfloat16).reshape(frames, patches, attn)


def per_device(
    frames_in,
    modulation,
    self_proj,
    self_out,
    cross_query,
    cross_keyval,
    cross_out,
    text_bank,
    prompt_pick,
    text_lengths,
):
    count = lax.axis_size("seq")
    frame_rows, pixels, width = frames_in.shape
    attn = self_out.shape[0]
    heads = attn // HEAD_DIM
    scale_q = 1.0 / math.sqrt(HEAD_DIM)
    pix_dev = pixels // count
    frames = frame_rows * count
    tokens = frames_in.astype(jnp.float32)
    normed = (layer_norm(tokens) * (1.0 + modulation[1]) + modulation[0]).astype(jnp.bfloat16)
    switched = lax.all_to_all(normed, "seq", split_axis=1, concat_axis=0, tiled=True)
    flat_pix = switched.reshape(-1, width)
    qkv = jnp.dot(
        flat_pix,
        lax.all_gather(self_proj, "seq", axis=1, tiled=True),
        preferred_element_type=jnp.float32,
    ).astype(jnp.bfloat16)
    qkv = qkv.reshape(frames, pix_dev, 3 * attn)
    out_self, query_weight, out_cross = (
        lax.all_gather(self_out, "seq", axis=1, tiled=True),
        lax.all_gather(cross_query, "seq", axis=1, tiled=True),
        lax.all_gather(cross_out, "seq", axis=1, tiled=True),
    )
    attended = temporal_attention(qkv, heads, attn, scale_q)
    returned = lax.all_to_all(attended, "seq", split_axis=0, concat_axis=1, tiled=True)
    self_term = jnp.dot(returned.reshape(-1, attn), out_self, preferred_element_type=jnp.float32)
    after_self = (tokens.reshape(-1, width) + modulation[2] * self_term).astype(jnp.bfloat16)
    pick = prompt_pick[0]
    memory = spread_2(text_bank[0], "seq", pick)
    own_columns = jnp.dot(memory, cross_keyval, preferred_element_type=jnp.float32).astype(
        jnp.bfloat16
    )
    keyval = lax.all_gather(own_columns, "seq", axis=1, tiled=True)
    text_len = keyval.shape[0]
    text_key = head_norm(keyval[:, :attn].astype(jnp.float32), heads).astype(jnp.bfloat16)
    text_value = keyval[:, attn:].reshape(text_len, heads, HEAD_DIM)
    slots = jnp.arange(text_lengths.shape[0], dtype=jnp.int32)
    length = jnp.sum(jnp.where(slots == pick, text_lengths, 0))
    live = jnp.arange(text_len, dtype=jnp.int32) < length
    text_query = jnp.dot(after_self, query_weight, preferred_element_type=jnp.float32)
    text_query = (head_norm(text_query, heads) * scale_q).astype(jnp.bfloat16)
    cross_scores = jnp.einsum(
        "thd,lhd->thl", text_query, text_key, preferred_element_type=jnp.float32
    )
    cross_weights = jnp.where(live, jnp.exp(cross_scores), 0.0)
    cross_total = jnp.sum(cross_weights, axis=-1)
    cross_probs = cross_weights.astype(jnp.bfloat16)
    cross_mix = jnp.einsum(
        "thl,lhd->thd", cross_probs, text_value, preferred_element_type=jnp.float32
    )
    crossed = (cross_mix / cross_total[..., None]).astype(jnp.bfloat16).reshape(-1, attn)
    cross_term = jnp.dot(crossed, out_cross, preferred_element_type=jnp.float32)
    frames_out = (after_self.astype(jnp.float32) + cross_term).astype(jnp.bfloat16)
    return frames_out.reshape(frame_rows, pixels, width)


MESH = pl.DeviceIdType.MESH
CLIPS, LEVELS, CORES = 4, 4, 2


def greet(peers):
    barrier = pltpu.get_barrier_semaphore()
    for peer in peers:
        pl.semaphore_signal(barrier, inc=1, device_id=peer, device_id_type=MESH)
    pl.semaphore_wait(barrier, len(peers))


def places():
    clip, seq = lax.axis_index("clip"), lax.axis_index("seq")
    level, core = seq // CORES, seq % CORES
    sibling = level * CORES + (1 - core)
    levels = [lax.rem(level + step, LEVELS) for step in range(1, LEVELS)]
    clips = [lax.rem(clip + step, CLIPS) for step in range(1, CLIPS)]
    return clip, seq, level, core, sibling, levels, clips


def remote(src, dst, send_sem, recv_sem, clip, seq):
    return pltpu.make_async_remote_copy(
        src_ref=src,
        dst_ref=dst,
        send_sem=send_sem,
        recv_sem=recv_sem,
        device_id=(clip, seq),
        device_id_type=MESH,
    )


SUBS = ((0, 64), (64, 48))
OUT_ROWS, QUERY_ROWS, PROJ_ROWS = 144, 80, 224
PACKED = OUT_ROWS + QUERY_ROWS + PROJ_ROWS
GRANT = 56 * 1024 * 1024


def gather_kernel(
    frames_ref, modulation_ref, pack_ref, memory_ref, mask_ref,
    tokens_ref, weights_ref, text_ref,
    normed_ref, blocks_ref, masked_ref, half_ref, held_ref, slots_ref, own_ref,
    block_send, block_recv, pack_send, pack_recv, local_sem, half_sem,
    slice_send, slice_recv, text_send, text_recv,
):
    clip, seq, level, core, sibling, levels, _ = places()
    peers = [lax.rem(seq + step, LEVELS * CORES) for step in range(1, LEVELS * CORES)]
    beside, across, diagonal = clip + 1 - 2 * (clip % 2), (clip + 2) % 4, 3 - clip
    greet([(clip, peer) for peer in peers] + [(beside, seq), (across, seq)])
    piece = pack_ref.shape[0] // CLIPS
    pieces = [clip, beside, across, diagonal]
    sends = []

    def rows(part, sub):
        start, size = SUBS[sub]
        return pl.ds(pl.multiple_of(part * piece + start, 16), size)

    def start(copy):
        copy.start()
        sends.append(copy)

    def weight(src, shard, part, sub, kind, other, to_clip, to_seq):
        return remote(
            src.at[rows(part, sub)], weights_ref.at[shard, rows(part, sub)],
            pack_send.at[sub, kind, other], pack_recv.at[sub, shard, part], to_clip, to_seq,
        )

    def arrived(shard, part, sub):
        view = weights_ref.at[shard, rows(part, sub)]
        pltpu.make_async_copy(view, view, pack_recv.at[sub, shard, part]).wait()

    def up(sub, source):
        return weight(
            pack_ref if source is None else weights_ref.at[source * CORES + core],
            seq if source is None else source * CORES + core, clip, sub, 0,
            level if source is None else source, clip, jnp.minimum(seq + CORES, LEVELS * CORES - 1),
        )

    def down(sub, source):
        return weight(
            pack_ref if source is None else weights_ref.at[source * CORES + core],
            seq if source is None else source * CORES + core, clip, sub, 1,
            level if source is None else source, clip, jnp.maximum(seq - CORES, 0),
        )

    def climb(sub, source, act):
        upward = level < LEVELS - 1
        downward = level > 0
        if source is not None:
            upward = jnp.logical_and(upward, source < level)
            downward = jnp.logical_and(downward, source > level)

        @pl.when(upward)
        def _():
            act(up(sub, source))

        @pl.when(downward)
        def _():
            act(down(sub, source))

    def spread(sub, source):
        shard = source * CORES + core
        src = weights_ref.at[shard]
        return [
            weight(src, shard, clip, sub, 2, source, beside, seq),
            weight(src, shard, clip, sub, 3, source, across, seq),
            weight(src, shard, clip, sub, 4, source, clip, sibling),
        ]

    def turn(sub, source):
        shard = source * CORES + core
        part, to = (across, beside) if sub == 0 else (beside, across)
        arrived(shard, part, sub)
        start(weight(weights_ref.at[shard], shard, part, sub, 5, source, to, seq))

    def pass_on(sub, source, part, kind):
        shard = source * CORES + core
        start(weight(weights_ref.at[shard], shard, part, sub, kind, source, clip, sibling))

    for sub in range(2):
        climb(sub, None, lambda copy: copy.start())
    local = [pltpu.make_async_copy(pack_ref, weights_ref.at[seq], local_sem.at[0])]
    local[0].start()

    masked_ref[...] = memory_ref[...] * mask_ref[...]
    half = held_ref.shape[0]
    swap = remote(
        masked_ref.at[pl.ds(pl.multiple_of((1 - core) * half, 16), half)], half_ref,
        half_sem.at[0], half_sem.at[1], clip, sibling,
    )
    start(swap)
    for sub in range(2):
        for n, part in enumerate(pieces):
            start(weight(pack_ref, seq, part, sub, 2 + n, level, clip, sibling))

    def step(sub, distance):
        for source, there in (
            (level - distance, level >= distance),
            (level + distance, level + distance < LEVELS),
        ):

            @pl.when(there)
            def _(source=source):
                arrived(source * CORES + core, clip, sub)
                climb(sub, source, lambda copy: copy.start())
                for copy in spread(sub, source):
                    copy.start()

    frame_rows, pixels, width = frames_ref.shape
    gain, shift = 1.0 + modulation_ref[1:2], modulation_ref[0:1]
    for frame in range(frame_rows):
        normed_ref[frame] = layer_norm(frames_ref[frame].astype(jnp.float32)) * gain + shift
    count = blocks_ref.shape[0]
    pix = pixels // count
    for to in range(count):
        block = normed_ref[:, to * pix : (to + 1) * pix].reshape(frame_rows * pix, width)
        blocks_ref[to] = block.astype(jnp.bfloat16)
    step(0, 1)
    local.append(pltpu.make_async_copy(blocks_ref.at[seq], tokens_ref.at[seq], local_sem.at[1]))
    local[1].start()
    for n, peer in enumerate(peers):
        start(remote(
            blocks_ref.at[peer], tokens_ref.at[seq], block_send.at[n], block_recv.at[seq], clip, peer
        ))

    swap.wait_recv()
    held_ref[...] = masked_ref[pl.ds(pl.multiple_of(core * half, 16), half)] + half_ref[...]
    size = half // LEVELS
    for n, other in enumerate(levels):
        start(remote(
            held_ref.at[pl.ds(pl.multiple_of(other * size, 16), size)], slots_ref.at[level],
            slice_send.at[n], slice_recv.at[level], clip, other * CORES + core,
        ))

    def text(src, place, index, to):
        start(remote(src, text_ref.at[place], text_send.at[index], text_recv.at[place], clip, to))

    def wait(ref, sem, place):
        pltpu.make_async_copy(ref.at[place], ref.at[place], sem.at[place]).wait()

    step(1, 1)
    step(0, 2)
    total = held_ref[pl.ds(pl.multiple_of(level * size, 16), size)]
    for other in levels:
        wait(slots_ref, slice_recv, other)
        total = total + slots_ref[other]
    own_ref[...] = total
    place = core * LEVELS + level
    local.append(pltpu.make_async_copy(own_ref, text_ref.at[place], local_sem.at[2]))
    local[2].start()
    for n, other in enumerate(levels):
        text(own_ref, place, n, other * CORES + core)
    text(own_ref, place, 3, sibling)
    step(1, 2)
    step(0, 3)
    step(1, 3)
    for sub in range(2):
        for source in levels:
            turn(sub, source)
    for n, other in enumerate(levels):
        wait(text_ref, text_recv, core * LEVELS + other)
        text(text_ref.at[core * LEVELS + other], core * LEVELS + other, 4 + n, sibling)
    for sub in range(2):
        turned, plain = (across, beside) if sub == 0 else (beside, across)
        for source in levels:
            pass_on(sub, source, turned, 6)
            arrived(source * CORES + core, plain, sub)
            pass_on(sub, source, plain, 7)
    for sub in range(2):
        for source in levels:
            arrived(source * CORES + core, diagonal, sub)
            pass_on(sub, source, diagonal, 8)
    for other in [level] + levels:
        for part in pieces:
            for sub in range(2):
                arrived(other * CORES + 1 - core, part, sub)
        wait(text_ref, text_recv, (1 - core) * LEVELS + other)
    for peer in peers:
        wait(tokens_ref, block_recv, peer)
    for copy in local:
        copy.wait()
    for sub in range(2):
        climb(sub, None, lambda copy: copy.wait_send())
        for source in levels:
            climb(sub, source, lambda copy: copy.wait_send())
            for copy in spread(sub, source):
                copy.wait_send()
    for copy in sends:
        copy.wait_send()


def gather(frames_in, modulation, pack, memory, mask):
    frame_rows, pixels, width = frames_in.shape
    count, kind, text = LEVELS * CORES, frames_in.dtype, memory.shape[0]
    dma = pltpu.SemaphoreType.DMA
    anywhere = pl.BlockSpec(memory_space=pl.ANY)
    vmem = pl.BlockSpec(memory_space=pltpu.VMEM)
    block, size = frame_rows * pixels // count, text // count
    return pl.pallas_call(
        gather_kernel,
        out_shape=(
            jax.ShapeDtypeStruct((count, block, width), kind),
            jax.ShapeDtypeStruct((count,) + pack.shape, kind),
            jax.ShapeDtypeStruct((count, size, width), kind),
        ),
        in_specs=[vmem, vmem, anywhere, vmem, vmem],
        out_specs=(anywhere,) * 3,
        scratch_shapes=[
            pltpu.VMEM((frame_rows, pixels, width), jnp.float32),
            pltpu.VMEM((count, block, width), kind),
            pltpu.VMEM((text, width), kind),
            pltpu.VMEM((text // CORES, width), kind),
            pltpu.VMEM((text // CORES, width), kind),
            pltpu.VMEM((LEVELS, size, width), kind),
            pltpu.VMEM((size, width), kind),
            dma((count - 1,)),
            dma((count,)),
            dma((2, 9, LEVELS)),
            dma((2, count, CLIPS)),
            dma((3,)),
            dma((2,)),
            dma((LEVELS - 1,)),
            dma((LEVELS,)),
            dma((7,)),
            dma((count,)),
        ],
        compiler_params=pltpu.CompilerParams(
            collective_id=0, has_side_effects=True, vmem_limit_bytes=GRANT
        ),
    )(frames_in, modulation, pack, memory, mask)


def return_kernel(blocks_ref, text_ref, tokens_ref, keyval_ref,
                  block_send, block_recv, text_send, text_recv, local_sem):
    clip, seq, level, core, sibling, levels, _ = places()
    peers = [lax.rem(seq + step, LEVELS * CORES) for step in range(1, LEVELS * CORES)]
    greet([(clip, peer) for peer in peers])
    own = [pltpu.make_async_copy(text_ref, keyval_ref.at[seq], local_sem.at[0]),
           pltpu.make_async_copy(blocks_ref.at[seq], tokens_ref.at[seq], local_sem.at[1])]
    for copy in own:
        copy.start()
    sends = []

    def text(src, shard, index, to):
        copy = remote(src, keyval_ref.at[shard], text_send.at[index], text_recv.at[shard], clip, to)
        copy.start()
        sends.append(copy)

    def arrived(ref, sem, shard):
        pltpu.make_async_copy(ref.at[shard], ref.at[shard], sem.at[shard]).wait()

    for n, other in enumerate(levels):
        text(text_ref, seq, n, other * CORES + core)
    for n, peer in enumerate(peers):
        copy = remote(
            blocks_ref.at[peer], tokens_ref.at[seq], block_send.at[n], block_recv.at[seq], clip, peer
        )
        copy.start()
        sends.append(copy)
    text(text_ref, seq, 3, sibling)
    for n, other in enumerate(levels):
        shard = other * CORES + core
        arrived(keyval_ref, text_recv, shard)
        text(keyval_ref.at[shard], shard, 4 + n, sibling)
    for other in [level] + levels:
        arrived(keyval_ref, text_recv, other * CORES + 1 - core)
    for peer in peers:
        arrived(tokens_ref, block_recv, peer)
    for copy in own:
        copy.wait()
    for copy in sends:
        copy.wait_send()


def give_back(blocks, text):
    count, dma = blocks.shape[0], pltpu.SemaphoreType.DMA
    anywhere = pl.BlockSpec(memory_space=pl.ANY)
    return pl.pallas_call(
        return_kernel,
        out_shape=(
            jax.ShapeDtypeStruct(blocks.shape, blocks.dtype),
            jax.ShapeDtypeStruct((count,) + text.shape, text.dtype),
        ),
        in_specs=[anywhere, anywhere],
        out_specs=(anywhere, anywhere),
        scratch_shapes=[dma((count - 1,)), dma((count,)), dma((7,)), dma((count,)), dma((2,))],
        compiler_params=pltpu.CompilerParams(collective_id=1, has_side_effects=True),
    )(blocks, text)


def nt(left, right):
    return lax.dot_general(
        left, right, (((1,), (1,)), ((), ())), preferred_element_type=jnp.float32
    )


def unit(values, axis):
    power = jnp.sum(values * values, axis=axis, keepdims=True) * (1.0 / HEAD_DIM)
    return values * lax.rsqrt(power + EPS)


def self_kernel(pix, tokens_ref, weights_ref, text_ref, keyval_ref, out_ref, text_out_ref, qkv_ref):
    tokens = tokens_ref[...]
    count = weights_ref.shape[0]
    per = 3
    heads = count * per // 3
    for shard in range(count):
        columns = nt(tokens, weights_ref[shard, OUT_ROWS + QUERY_ROWS :])
        for j in range(per):
            part = columns[:, j * HEAD_DIM : (j + 1) * HEAD_DIM]
            qkv_ref[shard * per + j] = part.astype(jnp.bfloat16)
    text_out_ref[...] = nt(keyval_ref[...], text_ref[...]).astype(jnp.bfloat16)
    rows = tokens.shape[0]
    row = lax.broadcasted_iota(jnp.int32, (rows, rows), 0)
    column = lax.broadcasted_iota(jnp.int32, (rows, rows), 1)
    same = (row % pix) == (column % pix)
    scale_q = 1.0 / math.sqrt(HEAD_DIM)
    outs = []
    for head in range(heads):
        query = (unit(qkv_ref[head].astype(jnp.float32), 1) * scale_q).astype(jnp.bfloat16)
        key = unit(qkv_ref[heads + head].astype(jnp.float32), 1).astype(jnp.bfloat16)
        weights = jnp.where(same, jnp.exp(nt(query, key)), 0.0)
        total = jnp.sum(weights, axis=1, keepdims=True)
        mixed = jnp.dot(
            weights.astype(jnp.bfloat16), qkv_ref[2 * heads + head],
            preferred_element_type=jnp.float32,
        )
        outs.append(mixed / total)
    pad = out_ref.shape[1] - heads * HEAD_DIM
    outs.append(jnp.zeros((rows, pad), jnp.float32))
    out_ref[...] = jnp.concatenate(outs, axis=1).astype(jnp.bfloat16)


def cross_kernel(
    returned_ref, frames_ref, modulation_ref, weights_ref, keyval_ref, pick_ref, lengths_ref, out_ref,
    attended_ref, out_weight_ref,
):
    count, block, lanes = returned_ref.shape
    frame_rows, pixels, width = frames_ref.shape
    pix = block // frame_rows
    for src in range(count):
        part = returned_ref[src].astype(jnp.float32)
        for frame in range(frame_rows):
            at = frame * pixels + src * pix
            attended_ref[at : at + pix] = part[frame * pix : (frame + 1) * pix]
        out_weight_ref[src * OUT_ROWS : (src + 1) * OUT_ROWS] = weights_ref[src, :OUT_ROWS]
    self_term = nt(attended_ref[...].astype(jnp.bfloat16), out_weight_ref[:, :lanes])
    tokens = frames_ref[...].astype(jnp.float32).reshape(frame_rows * pixels, width)
    after_self = (tokens + modulation_ref[2:3] * self_term).astype(jnp.bfloat16)
    text_len = keyval_ref.shape[2]
    live = lax.broadcasted_iota(jnp.int32, (1, text_len), 1) < lengths_ref[pick_ref[0]]
    heads = count
    scale_q = 1.0 / math.sqrt(HEAD_DIM)
    outs = [jnp.zeros((tokens.shape[0], lanes - heads * HEAD_DIM), jnp.float32)]
    per = keyval_ref.shape[1] // HEAD_DIM

    def of_head(index):
        shard = keyval_ref[index // per].astype(jnp.float32)
        return shard[(index % per) * HEAD_DIM : (index % per + 1) * HEAD_DIM]

    for head in range(heads):
        query = nt(after_self, weights_ref[head, OUT_ROWS : OUT_ROWS + QUERY_ROWS])
        query = (unit(query, 1) * scale_q).astype(jnp.bfloat16)[:, :HEAD_DIM]
        key = unit(of_head(head), 0).astype(jnp.bfloat16)
        scores = jnp.dot(query, key, preferred_element_type=jnp.float32)
        weights = jnp.where(live, jnp.exp(scores), 0.0)
        total = jnp.sum(weights, axis=1, keepdims=True)
        value = of_head(heads + head).astype(jnp.bfloat16)
        outs.append(nt(weights.astype(jnp.bfloat16), value) / total)
    crossed = jnp.concatenate(outs, axis=1).astype(jnp.bfloat16)
    cross_term = nt(crossed, out_weight_ref[:, width - lanes :])
    result = (after_self.astype(jnp.float32) + cross_term).astype(jnp.bfloat16)
    out_ref[...] = result.reshape(frame_rows, pixels, width)


def per_device_shared(
    frames_in,
    modulation,
    self_proj,
    self_out,
    cross_query,
    cross_keyval,
    cross_out,
    text_bank,
    prompt_pick,
    text_lengths,
):
    count = lax.axis_size("seq")
    frame_rows, pixels, width = frames_in.shape
    attn = self_out.shape[0]
    block = frame_rows * pixels // count
    lanes = -(-attn // 128) * 128
    pick = prompt_pick[0]
    memory = text_bank[0]
    text_len = memory.shape[0]
    mine = (lax.axis_index("seq") == pick).astype(jnp.bfloat16)
    mask = jnp.full((1, width), mine)

    def fill(part, rows):
        return jnp.pad(part, ((0, rows - part.shape[0]), (0, 0)))

    pack = jnp.concatenate(
        [
            jnp.concatenate([self_out.T, cross_out.T], axis=1),
            fill(cross_query.T, QUERY_ROWS),
            fill(self_proj.T, PROJ_ROWS),
        ],
        axis=0,
    )
    switched, weights, text = gather(frames_in, modulation, pack, memory, mask)
    attended, own_keyval = pl.pallas_call(
        functools.partial(self_kernel, pixels // count),
        out_shape=(
            jax.ShapeDtypeStruct((count * block, lanes), jnp.bfloat16),
            jax.ShapeDtypeStruct((cross_keyval.shape[1], text_len), jnp.bfloat16),
        ),
        scratch_shapes=[pltpu.VMEM((3 * attn // HEAD_DIM, count * block, HEAD_DIM), jnp.bfloat16)],
        compiler_params=pltpu.CompilerParams(vmem_limit_bytes=GRANT),
    )(switched.reshape(-1, width), weights, text.reshape(text_len, width), cross_keyval.T)
    returned, keyval = give_back(attended.reshape(count, block, lanes), own_keyval)
    return pl.pallas_call(
        cross_kernel,
        out_shape=jax.ShapeDtypeStruct(frames_in.shape, jnp.bfloat16),
        in_specs=[pl.BlockSpec(memory_space=pltpu.VMEM)] * 5
        + [pl.BlockSpec(memory_space=pltpu.SMEM)] * 2,
        scratch_shapes=[
            pltpu.VMEM((frame_rows * pixels, lanes), jnp.float32),
            pltpu.VMEM((count * OUT_ROWS, width), jnp.bfloat16),
        ],
        compiler_params=pltpu.CompilerParams(vmem_limit_bytes=GRANT),
    )(returned, frames_in, modulation, weights, keyval, prompt_pick, text_lengths)


def solution(mesh):
    shared = mesh.shape["clip"] == CLIPS and mesh.shape["seq"] == LEVELS * CORES
    placed = (
        P(("clip", "seq"), None, None),
        P("clip", None),
        P(None, "seq"),
        P(None, "seq"),
        P(None, "seq"),
        P(None, "seq"),
        P(None, "seq"),
        P("seq", None, None),
        P("clip"),
        P(),
    )
    return jax.shard_map(
        per_device_shared if shared else per_device,
        mesh=mesh,
        in_specs=placed,
        out_specs=P(("clip", "seq"), None, None),
        check_vma=False,
    )
```

```python
import math

import jax
import jax.numpy as jnp
from jax import lax
from jax.experimental import pallas as pl
from jax.experimental.pallas import tpu as pltpu
from jax.sharding import PartitionSpec as P

HEAD_DIM = 72


EPS = 1e-06


def spread_2(block, axis, owner):
    block = jnp.where(lax.axis_index(axis) == owner, block, jnp.zeros_like(block))
    return lax.psum(block, axis)


def layer_norm(values):
    mean = jnp.mean(values, axis=-1, keepdims=True)
    centred = values - mean
    spread = jnp.mean(centred * centred, axis=-1, keepdims=True)
    return centred * lax.rsqrt(spread + EPS)


def head_norm(values, heads):
    shaped = values.reshape(values.shape[:-1] + (heads, values.shape[-1] // heads))
    power = jnp.mean(shaped * shaped, axis=-1, keepdims=True)
    return shaped * lax.rsqrt(power + EPS)


def temporal_attention(qkv, heads, attn, scale_q):
    frames, patches = (qkv.shape[0], qkv.shape[1])
    query = (head_norm(qkv[..., :attn].astype(jnp.float32), heads) * scale_q).astype(jnp.bfloat16)
    key = head_norm(qkv[..., attn : 2 * attn].astype(jnp.float32), heads).astype(jnp.bfloat16)
    value = qkv[..., 2 * attn :].reshape(frames, patches, heads, attn // heads)
    scores = jnp.einsum("fphd,gphd->phfg", query, key, preferred_element_type=jnp.float32)
    weights = jnp.exp(scores)
    total = jnp.sum(weights, axis=-1)
    probs = weights.astype(jnp.bfloat16)
    mixed = jnp.einsum("phfg,gphd->fphd", probs, value, preferred_element_type=jnp.float32)
    attended = mixed / jnp.transpose(total, (2, 0, 1))[..., None]
    return attended.astype(jnp.bfloat16).reshape(frames, patches, attn)


def per_device(
    frames_in,
    modulation,
    self_proj,
    self_out,
    cross_query,
    cross_keyval,
    cross_out,
    text_bank,
    prompt_pick,
    text_lengths,
):
    count = lax.axis_size("seq")
    frame_rows, pixels, width = frames_in.shape
    attn = self_out.shape[0]
    heads = attn // HEAD_DIM
    scale_q = 1.0 / math.sqrt(HEAD_DIM)
    pix_dev = pixels // count
    frames = frame_rows * count
    tokens = frames_in.astype(jnp.float32)
    normed = (layer_norm(tokens) * (1.0 + modulation[1]) + modulation[0]).astype(jnp.bfloat16)
    switched = lax.all_to_all(normed, "seq", split_axis=1, concat_axis=0, tiled=True)
    flat_pix = switched.reshape(-1, width)
    qkv = jnp.dot(
        flat_pix,
        lax.all_gather(self_proj, "seq", axis=1, tiled=True),
        preferred_element_type=jnp.float32,
    ).astype(jnp.bfloat16)
    qkv = qkv.reshape(frames, pix_dev, 3 * attn)
    out_self, query_weight, out_cross = (
        lax.all_gather(self_out, "seq", axis=1, tiled=True),
        lax.all_gather(cross_query, "seq", axis=1, tiled=True),
        lax.all_gather(cross_out, "seq", axis=1, tiled=True),
    )
    attended = temporal_attention(qkv, heads, attn, scale_q)
    returned = lax.all_to_all(attended, "seq", split_axis=0, concat_axis=1, tiled=True)
    self_term = jnp.dot(returned.reshape(-1, attn), out_self, preferred_element_type=jnp.float32)
    after_self = (tokens.reshape(-1, width) + modulation[2] * self_term).astype(jnp.bfloat16)
    pick = prompt_pick[0]
    memory = spread_2(text_bank[0], "seq", pick)
    own_columns = jnp.dot(memory, cross_keyval, preferred_element_type=jnp.float32).astype(
        jnp.bfloat16
    )
    keyval = lax.all_gather(own_columns, "seq", axis=1, tiled=True)
    text_len = keyval.shape[0]
    text_key = head_norm(keyval[:, :attn].astype(jnp.float32), heads).astype(jnp.bfloat16)
    text_value = keyval[:, attn:].reshape(text_len, heads, HEAD_DIM)
    slots = jnp.arange(text_lengths.shape[0], dtype=jnp.int32)
    length = jnp.sum(jnp.where(slots == pick, text_lengths, 0))
    live = jnp.arange(text_len, dtype=jnp.int32) < length
    text_query = jnp.dot(after_self, query_weight, preferred_element_type=jnp.float32)
    text_query = (head_norm(text_query, heads) * scale_q).astype(jnp.bfloat16)
    cross_scores = jnp.einsum(
        "thd,lhd->thl", text_query, text_key, preferred_element_type=jnp.float32
    )
    cross_weights = jnp.where(live, jnp.exp(cross_scores), 0.0)
    cross_total = jnp.sum(cross_weights, axis=-1)
    cross_probs = cross_weights.astype(jnp.bfloat16)
    cross_mix = jnp.einsum(
        "thl,lhd->thd", cross_probs, text_value, preferred_element_type=jnp.float32
    )
    crossed = (cross_mix / cross_total[..., None]).astype(jnp.bfloat16).reshape(-1, attn)
    cross_term = jnp.dot(crossed, out_cross, preferred_element_type=jnp.float32)
    frames_out = (after_self.astype(jnp.float32) + cross_term).astype(jnp.bfloat16)
    return frames_out.reshape(frame_rows, pixels, width)


MESH = pl.DeviceIdType.MESH
CLIPS, LEVELS, CORES = 4, 4, 2


def greet(peers):
    barrier = pltpu.get_barrier_semaphore()
    for peer in peers:
        pl.semaphore_signal(barrier, inc=1, device_id=peer, device_id_type=MESH)
    pl.semaphore_wait(barrier, len(peers))


def places():
    clip, seq = lax.axis_index("clip"), lax.axis_index("seq")
    level, core = seq // CORES, seq % CORES
    sibling = level * CORES + (1 - core)
    levels = [lax.rem(level + step, LEVELS) for step in range(1, LEVELS)]
    clips = [lax.rem(clip + step, CLIPS) for step in range(1, CLIPS)]
    return clip, seq, level, core, sibling, levels, clips


def remote(src, dst, send_sem, recv_sem, clip, seq):
    return pltpu.make_async_remote_copy(
        src_ref=src,
        dst_ref=dst,
        send_sem=send_sem,
        recv_sem=recv_sem,
        device_id=(clip, seq),
        device_id_type=MESH,
    )


SUBS = ((0, 64), (64, 48))
PROJ_ROWS, OUT_ROWS, QUERY_ROWS = 224, 144, 80
GRANT = 56 * 1024 * 1024


def nt(left, right):
    return lax.dot_general(
        left, right, (((1,), (1,)), ((), ())), preferred_element_type=jnp.float32
    )


def unit(values, axis):
    power = jnp.sum(values * values, axis=axis, keepdims=True) * (1.0 / HEAD_DIM)
    return values * lax.rsqrt(power + EPS)


def project(tokens, weights_ref, qkv_ref):
    per = 3
    for shard in range(weights_ref.shape[0]):
        columns = nt(tokens, weights_ref[shard, :PROJ_ROWS])
        for j in range(per):
            part = columns[:, j * HEAD_DIM : (j + 1) * HEAD_DIM]
            qkv_ref[shard * per + j] = part.astype(jnp.bfloat16)


def self_head(qkv_ref, head, heads, pix):
    rows = qkv_ref.shape[1]
    row = lax.broadcasted_iota(jnp.int32, (rows, rows), 0)
    column = lax.broadcasted_iota(jnp.int32, (rows, rows), 1)
    same = (row % pix) == (column % pix)
    scale_q = 1.0 / math.sqrt(HEAD_DIM)
    query = (unit(qkv_ref[head].astype(jnp.float32), 1) * scale_q).astype(jnp.bfloat16)
    key = unit(qkv_ref[heads + head].astype(jnp.float32), 1).astype(jnp.bfloat16)
    weights = jnp.where(same, jnp.exp(nt(query, key)), 0.0)
    total = jnp.sum(weights, axis=1, keepdims=True)
    mixed = jnp.dot(
        weights.astype(jnp.bfloat16), qkv_ref[2 * heads + head],
        preferred_element_type=jnp.float32,
    )
    return mixed / total


def sublayers(
    returned_ref, frames_ref, modulation_ref, weights_ref, keyval_ref, pick_ref, lengths_ref,
    out_ref, attended_ref, out_weight_ref,
):
    count, block, lanes = returned_ref.shape
    frame_rows, pixels, width = frames_ref.shape
    pix = block // frame_rows
    for src in range(count):
        part = returned_ref[src].astype(jnp.float32)
        for frame in range(frame_rows):
            at = frame * pixels + src * pix
            attended_ref[at : at + pix] = part[frame * pix : (frame + 1) * pix]
        out_weight_ref[src * OUT_ROWS : (src + 1) * OUT_ROWS] = weights_ref[
            src, PROJ_ROWS : PROJ_ROWS + OUT_ROWS
        ]
    self_term = nt(attended_ref[...].astype(jnp.bfloat16), out_weight_ref[:, :lanes])
    tokens = frames_ref[...].astype(jnp.float32).reshape(frame_rows * pixels, width)
    after_self = (tokens + modulation_ref[2:3] * self_term).astype(jnp.bfloat16)
    text_len = keyval_ref.shape[2]
    live = lax.broadcasted_iota(jnp.int32, (1, text_len), 1) < lengths_ref[pick_ref[0]]
    heads = count
    scale_q = 1.0 / math.sqrt(HEAD_DIM)
    outs = [jnp.zeros((tokens.shape[0], lanes - heads * HEAD_DIM), jnp.float32)]
    per = keyval_ref.shape[1] // HEAD_DIM

    def of_head(index):
        shard = keyval_ref[index // per].astype(jnp.float32)
        return shard[(index % per) * HEAD_DIM : (index % per + 1) * HEAD_DIM]

    for head in range(heads):
        query = nt(after_self, weights_ref[head, PROJ_ROWS + OUT_ROWS :])
        query = (unit(query, 1) * scale_q).astype(jnp.bfloat16)[:, :HEAD_DIM]
        key = unit(of_head(head), 0).astype(jnp.bfloat16)
        scores = jnp.dot(query, key, preferred_element_type=jnp.float32)
        weights = jnp.where(live, jnp.exp(scores), 0.0)
        total = jnp.sum(weights, axis=1, keepdims=True)
        value = of_head(heads + head).astype(jnp.bfloat16)
        outs.append(nt(weights.astype(jnp.bfloat16), value) / total)
    crossed = jnp.concatenate(outs, axis=1).astype(jnp.bfloat16)
    cross_term = nt(crossed, out_weight_ref[:, width - lanes :])
    result = (after_self.astype(jnp.float32) + cross_term).astype(jnp.bfloat16)
    out_ref[...] = result.reshape(frame_rows, pixels, width)


def block_kernel(
    frames_ref, modulation_ref, pack_ref, memory_ref, mask_ref, text_weight_ref,
    pick_ref, lengths_ref,
    out_ref,
    tokens_ref, weights_ref, text_ref, qkv_ref, mixed_ref, returned_ref, columns_ref, keyval_ref,
    attended_ref, out_weight_ref,
    normed_ref, blocks_ref, masked_ref, half_ref, held_ref, slots_ref, own_ref,
    block_send, block_recv, pack_send, pack_recv, local_sem, half_sem,
    slice_send, slice_recv, text_send, text_recv,
    back_send, back_recv, keyval_send, keyval_recv,
):
    clip, seq, level, core, sibling, levels, _ = places()
    peers = [lax.rem(seq + step, LEVELS * CORES) for step in range(1, LEVELS * CORES)]
    beside, across, diagonal = clip + 1 - 2 * (clip % 2), (clip + 2) % 4, 3 - clip
    greet([(clip, peer) for peer in peers] + [(beside, seq), (across, seq)])
    pieces = [clip, beside, across, diagonal]
    sends = []

    def rows(part, sub):
        first, size = SUBS[sub]
        return pl.ds(pl.multiple_of(CLIPS * first + part * size, 16), size)

    def start(copy):
        copy.start()
        sends.append(copy)

    def weight(src, shard, part, sub, kind, other, to_clip, to_seq):
        return remote(
            src.at[rows(part, sub)], weights_ref.at[shard, rows(part, sub)],
            pack_send.at[sub, kind, other], pack_recv.at[sub, shard, part], to_clip, to_seq,
        )

    def arrived(shard, part, sub):
        view = weights_ref.at[shard, rows(part, sub)]
        pltpu.make_async_copy(view, view, pack_recv.at[sub, shard, part]).wait()

    def up(sub, source):
        return weight(
            pack_ref if source is None else weights_ref.at[source * CORES + core],
            seq if source is None else source * CORES + core, clip, sub, 0,
            level if source is None else source, clip, jnp.minimum(seq + CORES, LEVELS * CORES - 1),
        )

    def down(sub, source):
        return weight(
            pack_ref if source is None else weights_ref.at[source * CORES + core],
            seq if source is None else source * CORES + core, clip, sub, 1,
            level if source is None else source, clip, jnp.maximum(seq - CORES, 0),
        )

    def climb(sub, source, act):
        upward = level < LEVELS - 1
        downward = level > 0
        if source is not None:
            upward = jnp.logical_and(upward, source < level)
            downward = jnp.logical_and(downward, source > level)

        @pl.when(upward)
        def _():
            act(up(sub, source))

        @pl.when(downward)
        def _():
            act(down(sub, source))

    def spread(sub, source):
        shard = source * CORES + core
        src = weights_ref.at[shard]
        return [
            weight(src, shard, clip, sub, 2, source, beside, seq),
            weight(src, shard, clip, sub, 3, source, across, seq),
            weight(src, shard, clip, sub, 4, source, clip, sibling),
        ]

    def turn(sub, source):
        shard = source * CORES + core
        part, to = (across, beside) if sub == 0 else (beside, across)
        arrived(shard, part, sub)
        start(weight(weights_ref.at[shard], shard, part, sub, 5, source, to, seq))

    def pass_on(sub, source, part, kind):
        shard = source * CORES + core
        start(weight(weights_ref.at[shard], shard, part, sub, kind, source, clip, sibling))

    climb(0, None, lambda copy: copy.start())
    local = [pltpu.make_async_copy(pack_ref, weights_ref.at[seq], local_sem.at[0])]
    local[0].start()

    masked_ref[...] = memory_ref[...] * mask_ref[...]
    half = held_ref.shape[0]
    swap = remote(
        masked_ref.at[pl.ds(pl.multiple_of((1 - core) * half, 16), half)], half_ref,
        half_sem.at[0], half_sem.at[1], clip, sibling,
    )
    start(swap)

    def to_sibling(sub):
        for n, part in enumerate(pieces):
            start(weight(pack_ref, seq, part, sub, 2 + n, level, clip, sibling))

    to_sibling(0)

    def step(sub, distance):
        for source, there in (
            (level - distance, level >= distance),
            (level + distance, level + distance < LEVELS),
        ):

            @pl.when(there)
            def _(source=source):
                arrived(source * CORES + core, clip, sub)
                climb(sub, source, lambda copy: copy.start())
                for copy in spread(sub, source):
                    copy.start()

    frame_rows, pixels, width = frames_ref.shape
    gain, shift = 1.0 + modulation_ref[1:2], modulation_ref[0:1]
    for frame in range(frame_rows):
        normed_ref[frame] = layer_norm(frames_ref[frame].astype(jnp.float32)) * gain + shift
    count = blocks_ref.shape[0]
    pix = pixels // count
    for to in range(count):
        block = normed_ref[:, to * pix : (to + 1) * pix].reshape(frame_rows * pix, width)
        blocks_ref[to] = block.astype(jnp.bfloat16)
    step(0, 1)
    local.append(pltpu.make_async_copy(blocks_ref.at[seq], tokens_ref.at[seq], local_sem.at[1]))
    local[1].start()
    for n, peer in enumerate(peers):
        start(remote(
            blocks_ref.at[peer], tokens_ref.at[seq], block_send.at[n], block_recv.at[seq], clip, peer
        ))

    swap.wait_recv()
    held_ref[...] = masked_ref[pl.ds(pl.multiple_of(core * half, 16), half)] + half_ref[...]
    size = half // LEVELS
    for n, other in enumerate(levels):
        start(remote(
            held_ref.at[pl.ds(pl.multiple_of(other * size, 16), size)], slots_ref.at[level],
            slice_send.at[n], slice_recv.at[level], clip, other * CORES + core,
        ))

    def text(src, place, index, to):
        start(remote(src, text_ref.at[place], text_send.at[index], text_recv.at[place], clip, to))

    def wait(ref, sem, place):
        pltpu.make_async_copy(ref.at[place], ref.at[place], sem.at[place]).wait()

    step(0, 2)
    total = held_ref[pl.ds(pl.multiple_of(level * size, 16), size)]
    for other in levels:
        wait(slots_ref, slice_recv, other)
        total = total + slots_ref[other]
    own_ref[...] = total
    place = core * LEVELS + level
    local.append(pltpu.make_async_copy(own_ref, text_ref.at[place], local_sem.at[2]))
    local[2].start()
    for n, other in enumerate(levels):
        text(own_ref, place, n, other * CORES + core)
    text(own_ref, place, 3, sibling)
    step(0, 3)
    climb(1, None, lambda copy: copy.start())

    def finish(sub):
        turned, plain = (across, beside) if sub == 0 else (beside, across)
        for source in levels:
            turn(sub, source)
        for source in levels:
            pass_on(sub, source, turned, 6)
            arrived(source * CORES + core, plain, sub)
            pass_on(sub, source, plain, 7)
        for source in levels:
            arrived(source * CORES + core, diagonal, sub)
            pass_on(sub, source, diagonal, 8)

    def complete(sub):
        for other in [level] + levels:
            for part in pieces:
                arrived(other * CORES + 1 - core, part, sub)

    finish(0)
    to_sibling(1)
    for n, other in enumerate(levels):
        wait(text_ref, text_recv, core * LEVELS + other)
        text(text_ref.at[core * LEVELS + other], core * LEVELS + other, 4 + n, sibling)
    step(1, 1)
    for other in [level] + levels:
        wait(text_ref, text_recv, (1 - core) * LEVELS + other)
    local[2].wait()
    memory = text_ref[...].reshape(count * text_ref.shape[1], width)
    columns_ref[...] = nt(text_weight_ref[...], memory).astype(jnp.bfloat16)

    def keyval(src, shard, index, to):
        start(remote(
            src, keyval_ref.at[shard], keyval_send.at[index], keyval_recv.at[shard], clip, to
        ))

    local.append(pltpu.make_async_copy(columns_ref, keyval_ref.at[seq], local_sem.at[3]))
    local[3].start()
    for n, other in enumerate(levels):
        keyval(columns_ref, seq, n, other * CORES + core)
    keyval(columns_ref, seq, 3, sibling)
    complete(0)
    for peer in peers:
        wait(tokens_ref, block_recv, peer)
    local[0].wait()
    local[1].wait()
    project(tokens_ref[...].reshape(frame_rows * pixels, width), weights_ref, qkv_ref)
    step(1, 2)
    heads = qkv_ref.shape[0] // 3
    outs = [self_head(qkv_ref, head, heads, pix) for head in range(heads // 2)]
    step(1, 3)
    outs += [self_head(qkv_ref, head, heads, pix) for head in range(heads // 2, heads)]
    lanes = mixed_ref.shape[2]
    outs.append(jnp.zeros((frame_rows * pixels, lanes - heads * HEAD_DIM), jnp.float32))
    mixed = jnp.concatenate(outs, axis=1).astype(jnp.bfloat16)
    mixed_ref[...] = mixed.reshape(mixed_ref.shape)
    local.append(pltpu.make_async_copy(mixed_ref.at[seq], returned_ref.at[seq], local_sem.at[4]))
    local[4].start()
    for n, peer in enumerate(peers):
        start(remote(
            mixed_ref.at[peer], returned_ref.at[seq], back_send.at[n], back_recv.at[seq], clip, peer
        ))
    for n, other in enumerate(levels):
        shard = other * CORES + core
        wait(keyval_ref, keyval_recv, shard)
        keyval(keyval_ref.at[shard], shard, 4 + n, sibling)
    finish(1)
    complete(1)
    for other in [level] + levels:
        wait(keyval_ref, keyval_recv, other * CORES + 1 - core)
    for peer in peers:
        wait(returned_ref, back_recv, peer)
    local[3].wait()
    local[4].wait()
    sublayers(
        returned_ref, frames_ref, modulation_ref, weights_ref, keyval_ref, pick_ref, lengths_ref,
        out_ref, attended_ref, out_weight_ref,
    )
    for sub in range(2):
        climb(sub, None, lambda copy: copy.wait_send())
        for source in levels:
            climb(sub, source, lambda copy: copy.wait_send())
            for copy in spread(sub, source):
                copy.wait_send()
    for copy in sends:
        copy.wait_send()


def whole_block(frames_in, modulation, pack, memory, mask, text_weight, prompt_pick, text_lengths):
    frame_rows, pixels, width = frames_in.shape
    count, kind, text = LEVELS * CORES, frames_in.dtype, memory.shape[0]
    dma, vmem = pltpu.SemaphoreType.DMA, pl.BlockSpec(memory_space=pltpu.VMEM)
    smem = pl.BlockSpec(memory_space=pltpu.SMEM)
    tokens = frame_rows * pixels
    block, size, columns = tokens // count, text // count, text_weight.shape[0]
    heads = count
    lanes = -(-heads * HEAD_DIM // 128) * 128
    return pl.pallas_call(
        block_kernel,
        out_shape=jax.ShapeDtypeStruct(frames_in.shape, kind),
        in_specs=[vmem, vmem, vmem, vmem, vmem, vmem, smem, smem],
        out_specs=vmem,
        scratch_shapes=[
            pltpu.VMEM((count, block, width), kind),
            pltpu.VMEM((count,) + pack.shape, kind),
            pltpu.VMEM((count, size, width), kind),
            pltpu.VMEM((3 * heads, tokens, HEAD_DIM), kind),
            pltpu.VMEM((count, block, lanes), kind),
            pltpu.VMEM((count, block, lanes), kind),
            pltpu.VMEM((columns, text), kind),
            pltpu.VMEM((count, columns, text), kind),
            pltpu.VMEM((tokens, lanes), jnp.float32),
            pltpu.VMEM((count * OUT_ROWS, width), kind),
            pltpu.VMEM((frame_rows, pixels, width), jnp.float32),
            pltpu.VMEM((count, block, width), kind),
            pltpu.VMEM((text, width), kind),
            pltpu.VMEM((text // CORES, width), kind),
            pltpu.VMEM((text // CORES, width), kind),
            pltpu.VMEM((LEVELS, size, width), kind),
            pltpu.VMEM((size, width), kind),
            dma((count - 1,)),
            dma((count,)),
            dma((2, 9, LEVELS)),
            dma((2, count, CLIPS)),
            dma((5,)),
            dma((2,)),
            dma((LEVELS - 1,)),
            dma((LEVELS,)),
            dma((7,)),
            dma((count,)),
            dma((count - 1,)),
            dma((count,)),
            dma((7,)),
            dma((count,)),
        ],
        compiler_params=pltpu.CompilerParams(
            collective_id=0, has_side_effects=True, vmem_limit_bytes=GRANT
        ),
    )(frames_in, modulation, pack, memory, mask, text_weight, prompt_pick, text_lengths)


def per_device_shared(
    frames_in,
    modulation,
    self_proj,
    self_out,
    cross_query,
    cross_keyval,
    cross_out,
    text_bank,
    prompt_pick,
    text_lengths,
):
    pick = prompt_pick[0]
    memory = text_bank[0]
    mine = (lax.axis_index("seq") == pick).astype(jnp.bfloat16)
    mask = jnp.full((1, frames_in.shape[2]), mine)

    def fill(part, rows):
        return jnp.pad(part, ((0, rows - part.shape[0]), (0, 0)))

    pack = jnp.concatenate(
        [
            fill(self_proj.T, PROJ_ROWS),
            jnp.concatenate([self_out.T, cross_out.T], axis=1),
            fill(cross_query.T, QUERY_ROWS),
        ],
        axis=0,
    )
    return whole_block(
        frames_in, modulation, pack, memory, mask, cross_keyval.T, prompt_pick, text_lengths
    )


def solution(mesh):
    shared = mesh.shape["clip"] == CLIPS and mesh.shape["seq"] == LEVELS * CORES
    placed = (
        P(("clip", "seq"), None, None),
        P("clip", None),
        P(None, "seq"),
        P(None, "seq"),
        P(None, "seq"),
        P(None, "seq"),
        P(None, "seq"),
        P("seq", None, None),
        P("clip"),
        P(),
    )
    return jax.shard_map(
        per_device_shared if shared else per_device,
        mesh=mesh,
        in_specs=placed,
        out_specs=P(("clip", "seq"), None, None),
        check_vma=False,
    )
```

```python
import math

import jax
import jax.numpy as jnp
from jax import lax
from jax.experimental import pallas as pl
from jax.experimental.pallas import tpu as pltpu
from jax.sharding import PartitionSpec as P

HEAD_DIM = 72


EPS = 1e-06


def spread_2(block, axis, owner):
    block = jnp.where(lax.axis_index(axis) == owner, block, jnp.zeros_like(block))
    return lax.psum(block, axis)


def layer_norm(values):
    mean = jnp.mean(values, axis=-1, keepdims=True)
    centred = values - mean
    spread = jnp.mean(centred * centred, axis=-1, keepdims=True)
    return centred * lax.rsqrt(spread + EPS)


def head_norm(values, heads):
    shaped = values.reshape(values.shape[:-1] + (heads, values.shape[-1] // heads))
    power = jnp.mean(shaped * shaped, axis=-1, keepdims=True)
    return shaped * lax.rsqrt(power + EPS)


def temporal_attention(qkv, heads, attn, scale_q):
    frames, patches = (qkv.shape[0], qkv.shape[1])
    query = (head_norm(qkv[..., :attn].astype(jnp.float32), heads) * scale_q).astype(jnp.bfloat16)
    key = head_norm(qkv[..., attn : 2 * attn].astype(jnp.float32), heads).astype(jnp.bfloat16)
    value = qkv[..., 2 * attn :].reshape(frames, patches, heads, attn // heads)
    scores = jnp.einsum("fphd,gphd->phfg", query, key, preferred_element_type=jnp.float32)
    weights = jnp.exp(scores)
    total = jnp.sum(weights, axis=-1)
    probs = weights.astype(jnp.bfloat16)
    mixed = jnp.einsum("phfg,gphd->fphd", probs, value, preferred_element_type=jnp.float32)
    attended = mixed / jnp.transpose(total, (2, 0, 1))[..., None]
    return attended.astype(jnp.bfloat16).reshape(frames, patches, attn)


def per_device(
    frames_in,
    modulation,
    self_proj,
    self_out,
    cross_query,
    cross_keyval,
    cross_out,
    text_bank,
    prompt_pick,
    text_lengths,
):
    count = lax.axis_size("seq")
    frame_rows, pixels, width = frames_in.shape
    attn = self_out.shape[0]
    heads = attn // HEAD_DIM
    scale_q = 1.0 / math.sqrt(HEAD_DIM)
    pix_dev = pixels // count
    frames = frame_rows * count
    tokens = frames_in.astype(jnp.float32)
    normed = (layer_norm(tokens) * (1.0 + modulation[1]) + modulation[0]).astype(jnp.bfloat16)
    switched = lax.all_to_all(normed, "seq", split_axis=1, concat_axis=0, tiled=True)
    flat_pix = switched.reshape(-1, width)
    qkv = jnp.dot(
        flat_pix,
        lax.all_gather(self_proj, "seq", axis=1, tiled=True),
        preferred_element_type=jnp.float32,
    ).astype(jnp.bfloat16)
    qkv = qkv.reshape(frames, pix_dev, 3 * attn)
    out_self, query_weight, out_cross = (
        lax.all_gather(self_out, "seq", axis=1, tiled=True),
        lax.all_gather(cross_query, "seq", axis=1, tiled=True),
        lax.all_gather(cross_out, "seq", axis=1, tiled=True),
    )
    attended = temporal_attention(qkv, heads, attn, scale_q)
    returned = lax.all_to_all(attended, "seq", split_axis=0, concat_axis=1, tiled=True)
    self_term = jnp.dot(returned.reshape(-1, attn), out_self, preferred_element_type=jnp.float32)
    after_self = (tokens.reshape(-1, width) + modulation[2] * self_term).astype(jnp.bfloat16)
    pick = prompt_pick[0]
    memory = spread_2(text_bank[0], "seq", pick)
    own_columns = jnp.dot(memory, cross_keyval, preferred_element_type=jnp.float32).astype(
        jnp.bfloat16
    )
    keyval = lax.all_gather(own_columns, "seq", axis=1, tiled=True)
    text_len = keyval.shape[0]
    text_key = head_norm(keyval[:, :attn].astype(jnp.float32), heads).astype(jnp.bfloat16)
    text_value = keyval[:, attn:].reshape(text_len, heads, HEAD_DIM)
    slots = jnp.arange(text_lengths.shape[0], dtype=jnp.int32)
    length = jnp.sum(jnp.where(slots == pick, text_lengths, 0))
    live = jnp.arange(text_len, dtype=jnp.int32) < length
    text_query = jnp.dot(after_self, query_weight, preferred_element_type=jnp.float32)
    text_query = (head_norm(text_query, heads) * scale_q).astype(jnp.bfloat16)
    cross_scores = jnp.einsum(
        "thd,lhd->thl", text_query, text_key, preferred_element_type=jnp.float32
    )
    cross_weights = jnp.where(live, jnp.exp(cross_scores), 0.0)
    cross_total = jnp.sum(cross_weights, axis=-1)
    cross_probs = cross_weights.astype(jnp.bfloat16)
    cross_mix = jnp.einsum(
        "thl,lhd->thd", cross_probs, text_value, preferred_element_type=jnp.float32
    )
    crossed = (cross_mix / cross_total[..., None]).astype(jnp.bfloat16).reshape(-1, attn)
    cross_term = jnp.dot(crossed, out_cross, preferred_element_type=jnp.float32)
    frames_out = (after_self.astype(jnp.float32) + cross_term).astype(jnp.bfloat16)
    return frames_out.reshape(frame_rows, pixels, width)


MESH = pl.DeviceIdType.MESH
CLIPS, LEVELS, CORES = 4, 4, 2


def greet(peers):
    barrier = pltpu.get_barrier_semaphore()
    for peer in peers:
        pl.semaphore_signal(barrier, inc=1, device_id=peer, device_id_type=MESH)
    pl.semaphore_wait(barrier, len(peers))


def places():
    clip, seq = lax.axis_index("clip"), lax.axis_index("seq")
    level, core = seq // CORES, seq % CORES
    sibling = level * CORES + (1 - core)
    levels = [lax.rem(level + step, LEVELS) for step in range(1, LEVELS)]
    clips = [lax.rem(clip + step, CLIPS) for step in range(1, CLIPS)]
    return clip, seq, level, core, sibling, levels, clips


def remote(src, dst, send_sem, recv_sem, clip, seq):
    return pltpu.make_async_remote_copy(
        src_ref=src,
        dst_ref=dst,
        send_sem=send_sem,
        recv_sem=recv_sem,
        device_id=(clip, seq),
        device_id_type=MESH,
    )


SUBS = ((0, 64), (64, 48))
PROJ_ROWS, OUT_ROWS, QUERY_ROWS = 224, 144, 80
GRANT = 56 * 1024 * 1024


def nt(left, right):
    return lax.dot_general(
        left, right, (((1,), (1,)), ((), ())), preferred_element_type=jnp.float32
    )


def unit(values, axis):
    power = jnp.sum(values * values, axis=axis, keepdims=True) * (1.0 / HEAD_DIM)
    return values * lax.rsqrt(power + EPS)


def project(tokens, weights_ref, qkv_ref):
    per = 3
    for shard in range(weights_ref.shape[0]):
        columns = nt(tokens, weights_ref[shard, :PROJ_ROWS])
        for j in range(per):
            part = columns[:, j * HEAD_DIM : (j + 1) * HEAD_DIM]
            qkv_ref[shard * per + j] = part.astype(jnp.bfloat16)


def self_head(qkv_ref, head, heads, pix):
    rows = qkv_ref.shape[1]
    row = lax.broadcasted_iota(jnp.int32, (rows, rows), 0)
    column = lax.broadcasted_iota(jnp.int32, (rows, rows), 1)
    same = (row % pix) == (column % pix)
    scale_q = 1.0 / math.sqrt(HEAD_DIM)
    query = (unit(qkv_ref[head].astype(jnp.float32), 1) * scale_q).astype(jnp.bfloat16)
    key = unit(qkv_ref[heads + head].astype(jnp.float32), 1).astype(jnp.bfloat16)
    weights = jnp.where(same, jnp.exp(nt(query, key)), 0.0)
    total = jnp.sum(weights, axis=1, keepdims=True)
    mixed = jnp.dot(
        weights.astype(jnp.bfloat16), qkv_ref[2 * heads + head],
        preferred_element_type=jnp.float32,
    )
    return mixed / total


def assemble(weights_ref, out_weight_ref, query_weight_ref):
    outs = PROJ_ROWS + OUT_ROWS
    for src in range(weights_ref.shape[0]):
        out_weight_ref[src * OUT_ROWS : (src + 1) * OUT_ROWS] = weights_ref[src, PROJ_ROWS:outs]
        query_weight_ref[src * QUERY_ROWS : (src + 1) * QUERY_ROWS] = weights_ref[src, outs:]


def sublayers(
    returned_ref, frames_ref, modulation_ref, query_weight_ref, keyval_ref, pick_ref, lengths_ref,
    out_ref, attended_ref, out_weight_ref,
):
    count, block, lanes = returned_ref.shape
    frame_rows, pixels, width = frames_ref.shape
    pix = block // frame_rows
    for src in range(count):
        part = returned_ref[src].astype(jnp.float32)
        for frame in range(frame_rows):
            at = frame * pixels + src * pix
            attended_ref[at : at + pix] = part[frame * pix : (frame + 1) * pix]
    self_term = nt(attended_ref[...].astype(jnp.bfloat16), out_weight_ref[:, :lanes])
    tokens = frames_ref[...].astype(jnp.float32).reshape(frame_rows * pixels, width)
    after_self = (tokens + modulation_ref[2:3] * self_term).astype(jnp.bfloat16)
    text_len = keyval_ref.shape[2]
    live = lax.broadcasted_iota(jnp.int32, (1, text_len), 1) < lengths_ref[pick_ref[0]]
    heads = count
    scale_q = 1.0 / math.sqrt(HEAD_DIM)
    outs = [jnp.zeros((tokens.shape[0], lanes - heads * HEAD_DIM), jnp.float32)]
    per = keyval_ref.shape[1] // HEAD_DIM

    def of_head(index):
        shard = keyval_ref[index // per].astype(jnp.float32)
        return shard[(index % per) * HEAD_DIM : (index % per + 1) * HEAD_DIM]

    queries = nt(after_self, query_weight_ref[...])
    for head in range(heads):
        query = queries[:, head * QUERY_ROWS : head * QUERY_ROWS + HEAD_DIM]
        query = (unit(query, 1) * scale_q).astype(jnp.bfloat16)
        key = unit(of_head(head), 0).astype(jnp.bfloat16)
        scores = jnp.dot(query, key, preferred_element_type=jnp.float32)
        weights = jnp.where(live, jnp.exp(scores), 0.0)
        total = jnp.sum(weights, axis=1, keepdims=True)
        value = of_head(heads + head).astype(jnp.bfloat16)
        outs.append(nt(weights.astype(jnp.bfloat16), value) / total)
    crossed = jnp.concatenate(outs, axis=1).astype(jnp.bfloat16)
    cross_term = nt(crossed, out_weight_ref[:, width - lanes :])
    result = (after_self.astype(jnp.float32) + cross_term).astype(jnp.bfloat16)
    out_ref[...] = result.reshape(frame_rows, pixels, width)


def block_kernel(
    frames_ref, modulation_ref, pack_ref, memory_ref, mask_ref, text_weight_ref,
    pick_ref, lengths_ref,
    out_ref,
    tokens_ref, weights_ref, text_ref, qkv_ref, mixed_ref, returned_ref, columns_ref, keyval_ref,
    attended_ref, out_weight_ref, query_weight_ref,
    normed_ref, blocks_ref, masked_ref, half_ref, held_ref, slots_ref, own_ref,
    block_send, block_recv, pack_send, pack_recv, local_sem, half_sem,
    slice_send, slice_recv, text_send, text_recv,
    back_send, back_recv, keyval_send, keyval_recv,
):
    clip, seq, level, core, sibling, levels, _ = places()
    peers = [lax.rem(seq + step, LEVELS * CORES) for step in range(1, LEVELS * CORES)]
    beside, across, diagonal = clip + 1 - 2 * (clip % 2), (clip + 2) % 4, 3 - clip
    greet([(clip, peer) for peer in peers] + [(beside, seq), (across, seq)])
    pieces = [clip, beside, across, diagonal]
    sends = []

    def rows(part, sub):
        first, size = SUBS[sub]
        return pl.ds(pl.multiple_of(CLIPS * first + part * size, 16), size)

    def start(copy):
        copy.start()
        sends.append(copy)

    def weight(src, shard, part, sub, kind, other, to_clip, to_seq):
        return remote(
            src.at[rows(part, sub)], weights_ref.at[shard, rows(part, sub)],
            pack_send.at[sub, kind, other], pack_recv.at[sub, shard, part], to_clip, to_seq,
        )

    def arrived(shard, part, sub):
        view = weights_ref.at[shard, rows(part, sub)]
        pltpu.make_async_copy(view, view, pack_recv.at[sub, shard, part]).wait()

    def up(sub, source):
        return weight(
            pack_ref if source is None else weights_ref.at[source * CORES + core],
            seq if source is None else source * CORES + core, clip, sub, 0,
            level if source is None else source, clip, jnp.minimum(seq + CORES, LEVELS * CORES - 1),
        )

    def down(sub, source):
        return weight(
            pack_ref if source is None else weights_ref.at[source * CORES + core],
            seq if source is None else source * CORES + core, clip, sub, 1,
            level if source is None else source, clip, jnp.maximum(seq - CORES, 0),
        )

    def climb(sub, source, act):
        upward = level < LEVELS - 1
        downward = level > 0
        if source is not None:
            upward = jnp.logical_and(upward, source < level)
            downward = jnp.logical_and(downward, source > level)

        @pl.when(upward)
        def _():
            act(up(sub, source))

        @pl.when(downward)
        def _():
            act(down(sub, source))

    def spread(sub, source):
        shard = source * CORES + core
        src = weights_ref.at[shard]
        return [
            weight(src, shard, clip, sub, 2, source, beside, seq),
            weight(src, shard, clip, sub, 3, source, across, seq),
            weight(src, shard, clip, sub, 4, source, clip, sibling),
        ]

    def turn(sub, source):
        shard = source * CORES + core
        part, to = (across, beside) if sub == 0 else (beside, across)
        arrived(shard, part, sub)
        start(weight(weights_ref.at[shard], shard, part, sub, 5, source, to, seq))

    def pass_on(sub, source, part, kind):
        shard = source * CORES + core
        start(weight(weights_ref.at[shard], shard, part, sub, kind, source, clip, sibling))

    climb(0, None, lambda copy: copy.start())
    local = [pltpu.make_async_copy(pack_ref, weights_ref.at[seq], local_sem.at[0])]
    local[0].start()

    masked_ref[...] = memory_ref[...] * mask_ref[...]
    half = held_ref.shape[0]
    swap = remote(
        masked_ref.at[pl.ds(pl.multiple_of((1 - core) * half, 16), half)], half_ref,
        half_sem.at[0], half_sem.at[1], clip, sibling,
    )
    start(swap)

    def to_sibling(sub):
        for n, part in enumerate(pieces):
            start(weight(pack_ref, seq, part, sub, 2 + n, level, clip, sibling))

    to_sibling(0)

    def step(sub, distance):
        for source, there in (
            (level - distance, level >= distance),
            (level + distance, level + distance < LEVELS),
        ):

            @pl.when(there)
            def _(source=source):
                arrived(source * CORES + core, clip, sub)
                climb(sub, source, lambda copy: copy.start())
                for copy in spread(sub, source):
                    copy.start()

    frame_rows, pixels, width = frames_ref.shape
    gain, shift = 1.0 + modulation_ref[1:2], modulation_ref[0:1]
    for frame in range(frame_rows):
        normed_ref[frame] = layer_norm(frames_ref[frame].astype(jnp.float32)) * gain + shift
    count = blocks_ref.shape[0]
    pix = pixels // count
    for to in range(count):
        block = normed_ref[:, to * pix : (to + 1) * pix].reshape(frame_rows * pix, width)
        blocks_ref[to] = block.astype(jnp.bfloat16)
    step(0, 1)
    local.append(pltpu.make_async_copy(blocks_ref.at[seq], tokens_ref.at[seq], local_sem.at[1]))
    local[1].start()
    for n, peer in enumerate(peers):
        start(remote(
            blocks_ref.at[peer], tokens_ref.at[seq], block_send.at[n], block_recv.at[seq], clip, peer
        ))

    def text(src, place, index, to):
        start(remote(src, text_ref.at[place], text_send.at[index], text_recv.at[place], clip, to))

    def wait(ref, sem, place):
        pltpu.make_async_copy(ref.at[place], ref.at[place], sem.at[place]).wait()

    step(0, 2)
    step(0, 3)
    climb(1, None, lambda copy: copy.start())
    swap.wait_recv()
    held_ref[...] = masked_ref[pl.ds(pl.multiple_of(core * half, 16), half)] + half_ref[...]
    size = half // LEVELS
    for n, other in enumerate(levels):
        start(remote(
            held_ref.at[pl.ds(pl.multiple_of(other * size, 16), size)], slots_ref.at[level],
            slice_send.at[n], slice_recv.at[level], clip, other * CORES + core,
        ))

    def finish(sub):
        turned, plain = (across, beside) if sub == 0 else (beside, across)
        for source in levels:
            turn(sub, source)
        for source in levels:
            pass_on(sub, source, turned, 6)
            arrived(source * CORES + core, plain, sub)
            pass_on(sub, source, plain, 7)
        for source in levels:
            arrived(source * CORES + core, diagonal, sub)
            pass_on(sub, source, diagonal, 8)

    def complete(sub):
        for other in [level] + levels:
            for part in pieces:
                arrived(other * CORES + 1 - core, part, sub)

    finish(0)
    to_sibling(1)
    total = held_ref[pl.ds(pl.multiple_of(level * size, 16), size)]
    for other in levels:
        wait(slots_ref, slice_recv, other)
        total = total + slots_ref[other]
    own_ref[...] = total
    place = core * LEVELS + level
    local.append(pltpu.make_async_copy(own_ref, text_ref.at[place], local_sem.at[2]))
    local[2].start()
    for n, other in enumerate(levels):
        text(own_ref, place, n, other * CORES + core)
    text(own_ref, place, 3, sibling)
    step(1, 1)

    def keyval(src, shard, index, to):
        start(remote(
            src, keyval_ref.at[shard], keyval_send.at[index], keyval_recv.at[shard], clip, to
        ))

    complete(0)
    for peer in peers:
        wait(tokens_ref, block_recv, peer)
    local[0].wait()
    local[1].wait()
    project(tokens_ref[...].reshape(frame_rows * pixels, width), weights_ref, qkv_ref)
    for n, other in enumerate(levels):
        wait(text_ref, text_recv, core * LEVELS + other)
        text(text_ref.at[core * LEVELS + other], core * LEVELS + other, 4 + n, sibling)
    step(1, 2)
    heads = qkv_ref.shape[0] // 3
    outs = [self_head(qkv_ref, head, heads, pix) for head in range(heads // 2)]
    step(1, 3)
    for other in [level] + levels:
        wait(text_ref, text_recv, (1 - core) * LEVELS + other)
    local[2].wait()
    memory = text_ref[...].reshape(count * text_ref.shape[1], width)
    columns_ref[...] = nt(text_weight_ref[...], memory).astype(jnp.bfloat16)
    local.append(pltpu.make_async_copy(columns_ref, keyval_ref.at[seq], local_sem.at[3]))
    local[3].start()
    for n, other in enumerate(levels):
        keyval(columns_ref, seq, n, other * CORES + core)
    keyval(columns_ref, seq, 3, sibling)
    outs += [self_head(qkv_ref, head, heads, pix) for head in range(heads // 2, heads)]
    lanes = mixed_ref.shape[2]
    outs.append(jnp.zeros((frame_rows * pixels, lanes - heads * HEAD_DIM), jnp.float32))
    mixed = jnp.concatenate(outs, axis=1).astype(jnp.bfloat16)
    mixed_ref[...] = mixed.reshape(mixed_ref.shape)
    local.append(pltpu.make_async_copy(mixed_ref.at[seq], returned_ref.at[seq], local_sem.at[4]))
    local[4].start()
    for n, peer in enumerate(peers):
        start(remote(
            mixed_ref.at[peer], returned_ref.at[seq], back_send.at[n], back_recv.at[seq], clip, peer
        ))
    for n, other in enumerate(levels):
        shard = other * CORES + core
        wait(keyval_ref, keyval_recv, shard)
        keyval(keyval_ref.at[shard], shard, 4 + n, sibling)
    finish(1)
    complete(1)
    assemble(weights_ref, out_weight_ref, query_weight_ref)
    for other in [level] + levels:
        wait(keyval_ref, keyval_recv, other * CORES + 1 - core)
    for peer in peers:
        wait(returned_ref, back_recv, peer)
    local[3].wait()
    local[4].wait()
    sublayers(
        returned_ref, frames_ref, modulation_ref, query_weight_ref, keyval_ref, pick_ref,
        lengths_ref,
        out_ref, attended_ref, out_weight_ref,
    )
    for sub in range(2):
        climb(sub, None, lambda copy: copy.wait_send())
        for source in levels:
            climb(sub, source, lambda copy: copy.wait_send())
            for copy in spread(sub, source):
                copy.wait_send()
    for copy in sends:
        copy.wait_send()


def whole_block(frames_in, modulation, pack, memory, mask, text_weight, prompt_pick, text_lengths):
    frame_rows, pixels, width = frames_in.shape
    count, kind, text = LEVELS * CORES, frames_in.dtype, memory.shape[0]
    dma, vmem = pltpu.SemaphoreType.DMA, pl.BlockSpec(memory_space=pltpu.VMEM)
    smem = pl.BlockSpec(memory_space=pltpu.SMEM)
    tokens = frame_rows * pixels
    block, size, columns = tokens // count, text // count, text_weight.shape[0]
    heads = count
    lanes = -(-heads * HEAD_DIM // 128) * 128
    return pl.pallas_call(
        block_kernel,
        out_shape=jax.ShapeDtypeStruct(frames_in.shape, kind),
        in_specs=[vmem, vmem, vmem, vmem, vmem, vmem, smem, smem],
        out_specs=vmem,
        scratch_shapes=[
            pltpu.VMEM((count, block, width), kind),
            pltpu.VMEM((count,) + pack.shape, kind),
            pltpu.VMEM((count, size, width), kind),
            pltpu.VMEM((3 * heads, tokens, HEAD_DIM), kind),
            pltpu.VMEM((count, block, lanes), kind),
            pltpu.VMEM((count, block, lanes), kind),
            pltpu.VMEM((columns, text), kind),
            pltpu.VMEM((count, columns, text), kind),
            pltpu.VMEM((tokens, lanes), jnp.float32),
            pltpu.VMEM((count * OUT_ROWS, width), kind),
            pltpu.VMEM((count * QUERY_ROWS, width), kind),
            pltpu.VMEM((frame_rows, pixels, width), jnp.float32),
            pltpu.VMEM((count, block, width), kind),
            pltpu.VMEM((text, width), kind),
            pltpu.VMEM((text // CORES, width), kind),
            pltpu.VMEM((text // CORES, width), kind),
            pltpu.VMEM((LEVELS, size, width), kind),
            pltpu.VMEM((size, width), kind),
            dma((count - 1,)),
            dma((count,)),
            dma((2, 9, LEVELS)),
            dma((2, count, CLIPS)),
            dma((5,)),
            dma((2,)),
            dma((LEVELS - 1,)),
            dma((LEVELS,)),
            dma((7,)),
            dma((count,)),
            dma((count - 1,)),
            dma((count,)),
            dma((7,)),
            dma((count,)),
        ],
        compiler_params=pltpu.CompilerParams(
            collective_id=0, has_side_effects=True, vmem_limit_bytes=GRANT
        ),
    )(frames_in, modulation, pack, memory, mask, text_weight, prompt_pick, text_lengths)


def per_device_shared(
    frames_in,
    modulation,
    self_proj,
    self_out,
    cross_query,
    cross_keyval,
    cross_out,
    text_bank,
    prompt_pick,
    text_lengths,
):
    pick = prompt_pick[0]
    memory = text_bank[0]
    mine = (lax.axis_index("seq") == pick).astype(jnp.bfloat16)
    mask = jnp.full((1, frames_in.shape[2]), mine)

    def fill(part, rows):
        return jnp.pad(part, ((0, rows - part.shape[0]), (0, 0)))

    pack = jnp.concatenate(
        [
            fill(self_proj.T, PROJ_ROWS),
            jnp.concatenate([self_out.T, cross_out.T], axis=1),
            fill(cross_query.T, QUERY_ROWS),
        ],
        axis=0,
    )
    return whole_block(
        frames_in, modulation, pack, memory, mask, cross_keyval.T, prompt_pick, text_lengths
    )


def solution(mesh):
    shared = mesh.shape["clip"] == CLIPS and mesh.shape["seq"] == LEVELS * CORES
    placed = (
        P(("clip", "seq"), None, None),
        P("clip", None),
        P(None, "seq"),
        P(None, "seq"),
        P(None, "seq"),
        P(None, "seq"),
        P(None, "seq"),
        P("seq", None, None),
        P("clip"),
        P(),
    )
    return jax.shard_map(
        per_device_shared if shared else per_device,
        mesh=mesh,
        in_specs=placed,
        out_specs=P(("clip", "seq"), None, None),
        check_vma=False,
    )
```

```python
import math

import jax
import jax.numpy as jnp
from jax import lax
from jax.experimental import pallas as pl
from jax.experimental.pallas import tpu as pltpu
from jax.sharding import PartitionSpec as P

HEAD_DIM = 72


EPS = 1e-06


def spread_2(block, axis, owner):
    block = jnp.where(lax.axis_index(axis) == owner, block, jnp.zeros_like(block))
    return lax.psum(block, axis)


def layer_norm(values):
    mean = jnp.mean(values, axis=-1, keepdims=True)
    centred = values - mean
    spread = jnp.mean(centred * centred, axis=-1, keepdims=True)
    return centred * lax.rsqrt(spread + EPS)


def head_norm(values, heads):
    shaped = values.reshape(values.shape[:-1] + (heads, values.shape[-1] // heads))
    power = jnp.mean(shaped * shaped, axis=-1, keepdims=True)
    return shaped * lax.rsqrt(power + EPS)


def temporal_attention(qkv, heads, attn, scale_q):
    frames, patches = (qkv.shape[0], qkv.shape[1])
    query = (head_norm(qkv[..., :attn].astype(jnp.float32), heads) * scale_q).astype(jnp.bfloat16)
    key = head_norm(qkv[..., attn : 2 * attn].astype(jnp.float32), heads).astype(jnp.bfloat16)
    value = qkv[..., 2 * attn :].reshape(frames, patches, heads, attn // heads)
    scores = jnp.einsum("fphd,gphd->phfg", query, key, preferred_element_type=jnp.float32)
    weights = jnp.exp(scores)
    total = jnp.sum(weights, axis=-1)
    probs = weights.astype(jnp.bfloat16)
    mixed = jnp.einsum("phfg,gphd->fphd", probs, value, preferred_element_type=jnp.float32)
    attended = mixed / jnp.transpose(total, (2, 0, 1))[..., None]
    return attended.astype(jnp.bfloat16).reshape(frames, patches, attn)


def per_device(
    frames_in,
    modulation,
    self_proj,
    self_out,
    cross_query,
    cross_keyval,
    cross_out,
    text_bank,
    prompt_pick,
    text_lengths,
):
    count = lax.axis_size("seq")
    frame_rows, pixels, width = frames_in.shape
    attn = self_out.shape[0]
    heads = attn // HEAD_DIM
    scale_q = 1.0 / math.sqrt(HEAD_DIM)
    pix_dev = pixels // count
    frames = frame_rows * count
    tokens = frames_in.astype(jnp.float32)
    normed = (layer_norm(tokens) * (1.0 + modulation[1]) + modulation[0]).astype(jnp.bfloat16)
    switched = lax.all_to_all(normed, "seq", split_axis=1, concat_axis=0, tiled=True)
    flat_pix = switched.reshape(-1, width)
    qkv = jnp.dot(
        flat_pix,
        lax.all_gather(self_proj, "seq", axis=1, tiled=True),
        preferred_element_type=jnp.float32,
    ).astype(jnp.bfloat16)
    qkv = qkv.reshape(frames, pix_dev, 3 * attn)
    out_self, query_weight, out_cross = (
        lax.all_gather(self_out, "seq", axis=1, tiled=True),
        lax.all_gather(cross_query, "seq", axis=1, tiled=True),
        lax.all_gather(cross_out, "seq", axis=1, tiled=True),
    )
    attended = temporal_attention(qkv, heads, attn, scale_q)
    returned = lax.all_to_all(attended, "seq", split_axis=0, concat_axis=1, tiled=True)
    self_term = jnp.dot(returned.reshape(-1, attn), out_self, preferred_element_type=jnp.float32)
    after_self = (tokens.reshape(-1, width) + modulation[2] * self_term).astype(jnp.bfloat16)
    pick = prompt_pick[0]
    memory = spread_2(text_bank[0], "seq", pick)
    own_columns = jnp.dot(memory, cross_keyval, preferred_element_type=jnp.float32).astype(
        jnp.bfloat16
    )
    keyval = lax.all_gather(own_columns, "seq", axis=1, tiled=True)
    text_len = keyval.shape[0]
    text_key = head_norm(keyval[:, :attn].astype(jnp.float32), heads).astype(jnp.bfloat16)
    text_value = keyval[:, attn:].reshape(text_len, heads, HEAD_DIM)
    slots = jnp.arange(text_lengths.shape[0], dtype=jnp.int32)
    length = jnp.sum(jnp.where(slots == pick, text_lengths, 0))
    live = jnp.arange(text_len, dtype=jnp.int32) < length
    text_query = jnp.dot(after_self, query_weight, preferred_element_type=jnp.float32)
    text_query = (head_norm(text_query, heads) * scale_q).astype(jnp.bfloat16)
    cross_scores = jnp.einsum(
        "thd,lhd->thl", text_query, text_key, preferred_element_type=jnp.float32
    )
    cross_weights = jnp.where(live, jnp.exp(cross_scores), 0.0)
    cross_total = jnp.sum(cross_weights, axis=-1)
    cross_probs = cross_weights.astype(jnp.bfloat16)
    cross_mix = jnp.einsum(
        "thl,lhd->thd", cross_probs, text_value, preferred_element_type=jnp.float32
    )
    crossed = (cross_mix / cross_total[..., None]).astype(jnp.bfloat16).reshape(-1, attn)
    cross_term = jnp.dot(crossed, out_cross, preferred_element_type=jnp.float32)
    frames_out = (after_self.astype(jnp.float32) + cross_term).astype(jnp.bfloat16)
    return frames_out.reshape(frame_rows, pixels, width)


MESH = pl.DeviceIdType.MESH
CLIPS, LEVELS, CORES = 4, 4, 2


def greet(peers):
    barrier = pltpu.get_barrier_semaphore()
    for peer in peers:
        pl.semaphore_signal(barrier, inc=1, device_id=peer, device_id_type=MESH)
    pl.semaphore_wait(barrier, len(peers))


def places():
    clip, seq = lax.axis_index("clip"), lax.axis_index("seq")
    level, core = seq // CORES, seq % CORES
    sibling = level * CORES + (1 - core)
    levels = [lax.rem(level + step, LEVELS) for step in range(1, LEVELS)]
    clips = [lax.rem(clip + step, CLIPS) for step in range(1, CLIPS)]
    return clip, seq, level, core, sibling, levels, clips


def remote(src, dst, send_sem, recv_sem, clip, seq):
    return pltpu.make_async_remote_copy(
        src_ref=src,
        dst_ref=dst,
        send_sem=send_sem,
        recv_sem=recv_sem,
        device_id=(clip, seq),
        device_id_type=MESH,
    )


SUBS = ((0, 64), (64, 48))
PROJ_ROWS, OUT_ROWS, QUERY_ROWS = 224, 144, 80
GRANT = 56 * 1024 * 1024


def nt(left, right):
    return lax.dot_general(
        left, right, (((1,), (1,)), ((), ())), preferred_element_type=jnp.float32
    )


def unit(values, axis):
    power = jnp.sum(values * values, axis=axis, keepdims=True) * (1.0 / HEAD_DIM)
    return values * lax.rsqrt(power + EPS)


def project(tokens, weights_ref, qkv_ref):
    per = 3
    for shard in range(weights_ref.shape[0]):
        columns = nt(tokens, weights_ref[shard, :PROJ_ROWS])
        for j in range(per):
            part = columns[:, j * HEAD_DIM : (j + 1) * HEAD_DIM]
            qkv_ref[shard * per + j] = part.astype(jnp.bfloat16)


def self_head(qkv_ref, head, heads, pix):
    rows = qkv_ref.shape[1]
    row = lax.broadcasted_iota(jnp.int32, (rows, rows), 0)
    column = lax.broadcasted_iota(jnp.int32, (rows, rows), 1)
    same = (row % pix) == (column % pix)
    scale_q = 1.0 / math.sqrt(HEAD_DIM)
    query = (unit(qkv_ref[head].astype(jnp.float32), 1) * scale_q).astype(jnp.bfloat16)
    key = unit(qkv_ref[heads + head].astype(jnp.float32), 1).astype(jnp.bfloat16)
    weights = jnp.where(same, jnp.exp(nt(query, key)), 0.0)
    total = jnp.sum(weights, axis=1, keepdims=True)
    mixed = jnp.dot(
        weights.astype(jnp.bfloat16), qkv_ref[2 * heads + head],
        preferred_element_type=jnp.float32,
    )
    return mixed / total


def assemble(weights_ref, out_weight_ref, query_weight_ref):
    outs = PROJ_ROWS + OUT_ROWS
    for src in range(weights_ref.shape[0]):
        out_weight_ref[src * OUT_ROWS : (src + 1) * OUT_ROWS] = weights_ref[src, PROJ_ROWS:outs]
        query_weight_ref[src * QUERY_ROWS : (src + 1) * QUERY_ROWS] = weights_ref[src, outs:]


def sublayers(
    returned_ref, frames_ref, modulation_ref, query_weight_ref, keyval_ref, pick_ref, lengths_ref,
    out_ref, attended_ref, out_weight_ref,
):
    count, block, lanes = returned_ref.shape
    frame_rows, pixels, width = frames_ref.shape
    pix = block // frame_rows
    for src in range(count):
        part = returned_ref[src].astype(jnp.float32)
        for frame in range(frame_rows):
            at = frame * pixels + src * pix
            attended_ref[at : at + pix] = part[frame * pix : (frame + 1) * pix]
    self_term = nt(attended_ref[...].astype(jnp.bfloat16), out_weight_ref[:, :lanes])
    tokens = frames_ref[...].astype(jnp.float32).reshape(frame_rows * pixels, width)
    after_self = (tokens + modulation_ref[2:3] * self_term).astype(jnp.bfloat16)
    text_len = keyval_ref.shape[2]
    live = lax.broadcasted_iota(jnp.int32, (1, text_len), 1) < lengths_ref[pick_ref[0]]
    heads = count
    scale_q = 1.0 / math.sqrt(HEAD_DIM)
    outs = [jnp.zeros((tokens.shape[0], lanes - heads * HEAD_DIM), jnp.float32)]
    per = keyval_ref.shape[1] // HEAD_DIM

    def of_head(index):
        shard = keyval_ref[index // per].astype(jnp.float32)
        return shard[(index % per) * HEAD_DIM : (index % per + 1) * HEAD_DIM]

    queries = nt(after_self, query_weight_ref[...])
    for head in range(heads):
        query = queries[:, head * QUERY_ROWS : head * QUERY_ROWS + HEAD_DIM]
        query = (unit(query, 1) * scale_q).astype(jnp.bfloat16)
        key = unit(of_head(head), 0).astype(jnp.bfloat16)
        scores = jnp.dot(query, key, preferred_element_type=jnp.float32)
        weights = jnp.where(live, jnp.exp(scores), 0.0)
        total = jnp.sum(weights, axis=1, keepdims=True)
        value = of_head(heads + head).astype(jnp.bfloat16)
        outs.append(nt(weights.astype(jnp.bfloat16), value) / total)
    crossed = jnp.concatenate(outs, axis=1).astype(jnp.bfloat16)
    cross_term = nt(crossed, out_weight_ref[:, width - lanes :])
    result = (after_self.astype(jnp.float32) + cross_term).astype(jnp.bfloat16)
    out_ref[...] = result.reshape(frame_rows, pixels, width)


def block_kernel(
    frames_ref, modulation_ref, pack_ref, memory_ref, mask_ref, text_weight_ref,
    pick_ref, lengths_ref,
    out_ref,
    tokens_ref, weights_ref, text_ref, qkv_ref, mixed_ref, returned_ref, columns_ref, keyval_ref,
    attended_ref, out_weight_ref, query_weight_ref,
    normed_ref, blocks_ref, masked_ref, half_ref, held_ref, slots_ref, own_ref,
    block_send, block_recv, pack_send, pack_recv, local_sem, half_sem,
    slice_send, slice_recv, text_send, text_recv,
    back_send, back_recv, keyval_send, keyval_recv,
):
    clip, seq, level, core, sibling, levels, _ = places()
    peers = [lax.rem(seq + step, LEVELS * CORES) for step in range(1, LEVELS * CORES)]
    beside, across, diagonal = clip + 1 - 2 * (clip % 2), (clip + 2) % 4, 3 - clip
    greet([(clip, peer) for peer in peers] + [(beside, seq), (across, seq)])
    pieces = [clip, beside, across, diagonal]
    sends = []

    def rows(part, sub):
        first, size = SUBS[sub]
        return pl.ds(pl.multiple_of(CLIPS * first + part * size, 16), size)

    def start(copy):
        copy.start()
        sends.append(copy)

    def weight(src, shard, part, sub, kind, other, to_clip, to_seq):
        return remote(
            src.at[rows(part, sub)], weights_ref.at[shard, rows(part, sub)],
            pack_send.at[sub, kind, other], pack_recv.at[sub, shard, part], to_clip, to_seq,
        )

    def arrived(shard, part, sub):
        view = weights_ref.at[shard, rows(part, sub)]
        pltpu.make_async_copy(view, view, pack_recv.at[sub, shard, part]).wait()

    def up(sub, source):
        return weight(
            pack_ref if source is None else weights_ref.at[source * CORES + core],
            seq if source is None else source * CORES + core, clip, sub, 0,
            level if source is None else source, clip, jnp.minimum(seq + CORES, LEVELS * CORES - 1),
        )

    def down(sub, source):
        return weight(
            pack_ref if source is None else weights_ref.at[source * CORES + core],
            seq if source is None else source * CORES + core, clip, sub, 1,
            level if source is None else source, clip, jnp.maximum(seq - CORES, 0),
        )

    def climb(sub, source, act):
        upward = level < LEVELS - 1
        downward = level > 0
        if source is not None:
            upward = jnp.logical_and(upward, source < level)
            downward = jnp.logical_and(downward, source > level)

        @pl.when(upward)
        def _():
            act(up(sub, source))

        @pl.when(downward)
        def _():
            act(down(sub, source))

    def spread(sub, source):
        shard = source * CORES + core
        src = weights_ref.at[shard]
        return [
            weight(src, shard, clip, sub, 2, source, beside, seq),
            weight(src, shard, clip, sub, 3, source, across, seq),
            weight(src, shard, clip, sub, 4, source, clip, sibling),
        ]

    def turn(sub, source):
        shard = source * CORES + core
        part, to = (across, beside) if sub == 0 else (beside, across)
        arrived(shard, part, sub)
        start(weight(weights_ref.at[shard], shard, part, sub, 5, source, to, seq))

    def pass_on(sub, source, part, kind):
        shard = source * CORES + core
        start(weight(weights_ref.at[shard], shard, part, sub, kind, source, clip, sibling))

    climb(0, None, lambda copy: copy.start())
    local = [pltpu.make_async_copy(pack_ref, weights_ref.at[seq], local_sem.at[0])]
    local[0].start()

    masked_ref[...] = memory_ref[...] * mask_ref[...]
    half = held_ref.shape[0]
    swap = remote(
        masked_ref.at[pl.ds(pl.multiple_of((1 - core) * half, 16), half)], half_ref,
        half_sem.at[0], half_sem.at[1], clip, sibling,
    )
    start(swap)

    def to_sibling(sub):
        for n, part in enumerate(pieces):
            start(weight(pack_ref, seq, part, sub, 2 + n, level, clip, sibling))

    to_sibling(0)

    def step(sub, distance):
        for source, there in (
            (level - distance, level >= distance),
            (level + distance, level + distance < LEVELS),
        ):

            @pl.when(there)
            def _(source=source):
                arrived(source * CORES + core, clip, sub)
                climb(sub, source, lambda copy: copy.start())
                for copy in spread(sub, source):
                    copy.start()

    frame_rows, pixels, width = frames_ref.shape
    gain, shift = 1.0 + modulation_ref[1:2], modulation_ref[0:1]
    for frame in range(frame_rows):
        normed_ref[frame] = layer_norm(frames_ref[frame].astype(jnp.float32)) * gain + shift
    count = blocks_ref.shape[0]
    pix = pixels // count
    for to in range(count):
        block = normed_ref[:, to * pix : (to + 1) * pix].reshape(frame_rows * pix, width)
        blocks_ref[to] = block.astype(jnp.bfloat16)
    step(0, 1)
    local.append(pltpu.make_async_copy(blocks_ref.at[seq], tokens_ref.at[seq], local_sem.at[1]))
    local[1].start()
    for n, peer in enumerate(peers):
        start(remote(
            blocks_ref.at[peer], tokens_ref.at[seq], block_send.at[n], block_recv.at[seq], clip, peer
        ))

    def text(src, place, index, to):
        start(remote(src, text_ref.at[place], text_send.at[index], text_recv.at[place], clip, to))

    def wait(ref, sem, place):
        pltpu.make_async_copy(ref.at[place], ref.at[place], sem.at[place]).wait()

    step(0, 2)
    step(0, 3)
    climb(1, None, lambda copy: copy.start())
    swap.wait_recv()
    held_ref[...] = masked_ref[pl.ds(pl.multiple_of(core * half, 16), half)] + half_ref[...]
    size = half // LEVELS
    for n, other in enumerate(levels):
        start(remote(
            held_ref.at[pl.ds(pl.multiple_of(other * size, 16), size)], slots_ref.at[level],
            slice_send.at[n], slice_recv.at[level], clip, other * CORES + core,
        ))

    def turn_all(sub):
        for source in levels:
            turn(sub, source)

    def beside_all(sub):
        turned, plain = (across, beside) if sub == 0 else (beside, across)
        for source in levels:
            pass_on(sub, source, turned, 6)
            arrived(source * CORES + core, plain, sub)
            pass_on(sub, source, plain, 7)

    def diagonal_all(sub):
        for source in levels:
            arrived(source * CORES + core, diagonal, sub)
            pass_on(sub, source, diagonal, 8)

    def complete(sub):
        for other in [level] + levels:
            for part in pieces:
                arrived(other * CORES + 1 - core, part, sub)

    turn_all(0)
    beside_all(0)
    step(1, 1)
    diagonal_all(0)
    to_sibling(1)
    total = held_ref[pl.ds(pl.multiple_of(level * size, 16), size)]
    for other in levels:
        wait(slots_ref, slice_recv, other)
        total = total + slots_ref[other]
    own_ref[...] = total
    place = core * LEVELS + level
    local.append(pltpu.make_async_copy(own_ref, text_ref.at[place], local_sem.at[2]))
    local[2].start()
    for n, other in enumerate(levels):
        text(own_ref, place, n, other * CORES + core)
    text(own_ref, place, 3, sibling)

    def keyval(src, shard, index, to):
        start(remote(
            src, keyval_ref.at[shard], keyval_send.at[index], keyval_recv.at[shard], clip, to
        ))

    step(1, 2)
    complete(0)
    for peer in peers:
        wait(tokens_ref, block_recv, peer)
    local[0].wait()
    local[1].wait()
    project(tokens_ref[...].reshape(frame_rows * pixels, width), weights_ref, qkv_ref)
    step(1, 3)
    for n, other in enumerate(levels):
        wait(text_ref, text_recv, core * LEVELS + other)
        text(text_ref.at[core * LEVELS + other], core * LEVELS + other, 4 + n, sibling)
    heads = qkv_ref.shape[0] // 3
    outs = [self_head(qkv_ref, head, heads, pix) for head in range(heads // 2)]
    turn_all(1)
    for other in [level] + levels:
        wait(text_ref, text_recv, (1 - core) * LEVELS + other)
    local[2].wait()
    memory = text_ref[...].reshape(count * text_ref.shape[1], width)
    columns_ref[...] = nt(text_weight_ref[...], memory).astype(jnp.bfloat16)
    local.append(pltpu.make_async_copy(columns_ref, keyval_ref.at[seq], local_sem.at[3]))
    local[3].start()
    for n, other in enumerate(levels):
        keyval(columns_ref, seq, n, other * CORES + core)
    keyval(columns_ref, seq, 3, sibling)
    outs += [self_head(qkv_ref, head, heads, pix) for head in range(heads // 2, heads)]
    lanes = mixed_ref.shape[2]
    outs.append(jnp.zeros((frame_rows * pixels, lanes - heads * HEAD_DIM), jnp.float32))
    mixed = jnp.concatenate(outs, axis=1).astype(jnp.bfloat16)
    mixed_ref[...] = mixed.reshape(mixed_ref.shape)
    local.append(pltpu.make_async_copy(mixed_ref.at[seq], returned_ref.at[seq], local_sem.at[4]))
    local[4].start()
    for n, peer in enumerate(peers):
        start(remote(
            mixed_ref.at[peer], returned_ref.at[seq], back_send.at[n], back_recv.at[seq], clip, peer
        ))
    beside_all(1)
    diagonal_all(1)
    for n, other in enumerate(levels):
        shard = other * CORES + core
        wait(keyval_ref, keyval_recv, shard)
        keyval(keyval_ref.at[shard], shard, 4 + n, sibling)
    complete(1)
    assemble(weights_ref, out_weight_ref, query_weight_ref)
    for other in [level] + levels:
        wait(keyval_ref, keyval_recv, other * CORES + 1 - core)
    for peer in peers:
        wait(returned_ref, back_recv, peer)
    local[3].wait()
    local[4].wait()
    sublayers(
        returned_ref, frames_ref, modulation_ref, query_weight_ref, keyval_ref, pick_ref,
        lengths_ref,
        out_ref, attended_ref, out_weight_ref,
    )
    for sub in range(2):
        climb(sub, None, lambda copy: copy.wait_send())
        for source in levels:
            climb(sub, source, lambda copy: copy.wait_send())
            for copy in spread(sub, source):
                copy.wait_send()
    for copy in sends:
        copy.wait_send()


def whole_block(frames_in, modulation, pack, memory, mask, text_weight, prompt_pick, text_lengths):
    frame_rows, pixels, width = frames_in.shape
    count, kind, text = LEVELS * CORES, frames_in.dtype, memory.shape[0]
    dma, vmem = pltpu.SemaphoreType.DMA, pl.BlockSpec(memory_space=pltpu.VMEM)
    smem = pl.BlockSpec(memory_space=pltpu.SMEM)
    tokens = frame_rows * pixels
    block, size, columns = tokens // count, text // count, text_weight.shape[0]
    heads = count
    lanes = -(-heads * HEAD_DIM // 128) * 128
    return pl.pallas_call(
        block_kernel,
        out_shape=jax.ShapeDtypeStruct(frames_in.shape, kind),
        in_specs=[vmem, vmem, vmem, vmem, vmem, vmem, smem, smem],
        out_specs=vmem,
        scratch_shapes=[
            pltpu.VMEM((count, block, width), kind),
            pltpu.VMEM((count,) + pack.shape, kind),
            pltpu.VMEM((count, size, width), kind),
            pltpu.VMEM((3 * heads, tokens, HEAD_DIM), kind),
            pltpu.VMEM((count, block, lanes), kind),
            pltpu.VMEM((count, block, lanes), kind),
            pltpu.VMEM((columns, text), kind),
            pltpu.VMEM((count, columns, text), kind),
            pltpu.VMEM((tokens, lanes), jnp.float32),
            pltpu.VMEM((count * OUT_ROWS, width), kind),
            pltpu.VMEM((count * QUERY_ROWS, width), kind),
            pltpu.VMEM((frame_rows, pixels, width), jnp.float32),
            pltpu.VMEM((count, block, width), kind),
            pltpu.VMEM((text, width), kind),
            pltpu.VMEM((text // CORES, width), kind),
            pltpu.VMEM((text // CORES, width), kind),
            pltpu.VMEM((LEVELS, size, width), kind),
            pltpu.VMEM((size, width), kind),
            dma((count - 1,)),
            dma((count,)),
            dma((2, 9, LEVELS)),
            dma((2, count, CLIPS)),
            dma((5,)),
            dma((2,)),
            dma((LEVELS - 1,)),
            dma((LEVELS,)),
            dma((7,)),
            dma((count,)),
            dma((count - 1,)),
            dma((count,)),
            dma((7,)),
            dma((count,)),
        ],
        compiler_params=pltpu.CompilerParams(
            collective_id=0, has_side_effects=True, vmem_limit_bytes=GRANT
        ),
    )(frames_in, modulation, pack, memory, mask, text_weight, prompt_pick, text_lengths)


def per_device_shared(
    frames_in,
    modulation,
    self_proj,
    self_out,
    cross_query,
    cross_keyval,
    cross_out,
    text_bank,
    prompt_pick,
    text_lengths,
):
    pick = prompt_pick[0]
    memory = text_bank[0]
    mine = (lax.axis_index("seq") == pick).astype(jnp.bfloat16)
    mask = jnp.full((1, frames_in.shape[2]), mine)

    def fill(part, rows):
        return jnp.pad(part, ((0, rows - part.shape[0]), (0, 0)))

    pack = jnp.concatenate(
        [
            fill(self_proj.T, PROJ_ROWS),
            jnp.concatenate([self_out.T, cross_out.T], axis=1),
            fill(cross_query.T, QUERY_ROWS),
        ],
        axis=0,
    )
    return whole_block(
        frames_in, modulation, pack, memory, mask, cross_keyval.T, prompt_pick, text_lengths
    )


def solution(mesh):
    shared = mesh.shape["clip"] == CLIPS and mesh.shape["seq"] == LEVELS * CORES
    placed = (
        P(("clip", "seq"), None, None),
        P("clip", None),
        P(None, "seq"),
        P(None, "seq"),
        P(None, "seq"),
        P(None, "seq"),
        P(None, "seq"),
        P("seq", None, None),
        P("clip"),
        P(),
    )
    return jax.shard_map(
        per_device_shared if shared else per_device,
        mesh=mesh,
        in_specs=placed,
        out_specs=P(("clip", "seq"), None, None),
        check_vma=False,
    )
```

```python
import math

import jax
import jax.numpy as jnp
from jax import lax
from jax.experimental import pallas as pl
from jax.experimental.pallas import tpu as pltpu
from jax.sharding import PartitionSpec as P

HEAD_DIM = 72


EPS = 1e-06


def spread_2(block, axis, owner):
    block = jnp.where(lax.axis_index(axis) == owner, block, jnp.zeros_like(block))
    return lax.psum(block, axis)


def layer_norm(values):
    mean = jnp.mean(values, axis=-1, keepdims=True)
    centred = values - mean
    spread = jnp.mean(centred * centred, axis=-1, keepdims=True)
    return centred * lax.rsqrt(spread + EPS)


def head_norm(values, heads):
    shaped = values.reshape(values.shape[:-1] + (heads, values.shape[-1] // heads))
    power = jnp.mean(shaped * shaped, axis=-1, keepdims=True)
    return shaped * lax.rsqrt(power + EPS)


def temporal_attention(qkv, heads, attn, scale_q):
    frames, patches = (qkv.shape[0], qkv.shape[1])
    query = (head_norm(qkv[..., :attn].astype(jnp.float32), heads) * scale_q).astype(jnp.bfloat16)
    key = head_norm(qkv[..., attn : 2 * attn].astype(jnp.float32), heads).astype(jnp.bfloat16)
    value = qkv[..., 2 * attn :].reshape(frames, patches, heads, attn // heads)
    scores = jnp.einsum("fphd,gphd->phfg", query, key, preferred_element_type=jnp.float32)
    weights = jnp.exp(scores)
    total = jnp.sum(weights, axis=-1)
    probs = weights.astype(jnp.bfloat16)
    mixed = jnp.einsum("phfg,gphd->fphd", probs, value, preferred_element_type=jnp.float32)
    attended = mixed / jnp.transpose(total, (2, 0, 1))[..., None]
    return attended.astype(jnp.bfloat16).reshape(frames, patches, attn)


def per_device(
    frames_in,
    modulation,
    self_proj,
    self_out,
    cross_query,
    cross_keyval,
    cross_out,
    text_bank,
    prompt_pick,
    text_lengths,
):
    count = lax.axis_size("seq")
    frame_rows, pixels, width = frames_in.shape
    attn = self_out.shape[0]
    heads = attn // HEAD_DIM
    scale_q = 1.0 / math.sqrt(HEAD_DIM)
    pix_dev = pixels // count
    frames = frame_rows * count
    tokens = frames_in.astype(jnp.float32)
    normed = (layer_norm(tokens) * (1.0 + modulation[1]) + modulation[0]).astype(jnp.bfloat16)
    switched = lax.all_to_all(normed, "seq", split_axis=1, concat_axis=0, tiled=True)
    flat_pix = switched.reshape(-1, width)
    qkv = jnp.dot(
        flat_pix,
        lax.all_gather(self_proj, "seq", axis=1, tiled=True),
        preferred_element_type=jnp.float32,
    ).astype(jnp.bfloat16)
    qkv = qkv.reshape(frames, pix_dev, 3 * attn)
    out_self, query_weight, out_cross = (
        lax.all_gather(self_out, "seq", axis=1, tiled=True),
        lax.all_gather(cross_query, "seq", axis=1, tiled=True),
        lax.all_gather(cross_out, "seq", axis=1, tiled=True),
    )
    attended = temporal_attention(qkv, heads, attn, scale_q)
    returned = lax.all_to_all(attended, "seq", split_axis=0, concat_axis=1, tiled=True)
    self_term = jnp.dot(returned.reshape(-1, attn), out_self, preferred_element_type=jnp.float32)
    after_self = (tokens.reshape(-1, width) + modulation[2] * self_term).astype(jnp.bfloat16)
    pick = prompt_pick[0]
    memory = spread_2(text_bank[0], "seq", pick)
    own_columns = jnp.dot(memory, cross_keyval, preferred_element_type=jnp.float32).astype(
        jnp.bfloat16
    )
    keyval = lax.all_gather(own_columns, "seq", axis=1, tiled=True)
    text_len = keyval.shape[0]
    text_key = head_norm(keyval[:, :attn].astype(jnp.float32), heads).astype(jnp.bfloat16)
    text_value = keyval[:, attn:].reshape(text_len, heads, HEAD_DIM)
    slots = jnp.arange(text_lengths.shape[0], dtype=jnp.int32)
    length = jnp.sum(jnp.where(slots == pick, text_lengths, 0))
    live = jnp.arange(text_len, dtype=jnp.int32) < length
    text_query = jnp.dot(after_self, query_weight, preferred_element_type=jnp.float32)
    text_query = (head_norm(text_query, heads) * scale_q).astype(jnp.bfloat16)
    cross_scores = jnp.einsum(
        "thd,lhd->thl", text_query, text_key, preferred_element_type=jnp.float32
    )
    cross_weights = jnp.where(live, jnp.exp(cross_scores), 0.0)
    cross_total = jnp.sum(cross_weights, axis=-1)
    cross_probs = cross_weights.astype(jnp.bfloat16)
    cross_mix = jnp.einsum(
        "thl,lhd->thd", cross_probs, text_value, preferred_element_type=jnp.float32
    )
    crossed = (cross_mix / cross_total[..., None]).astype(jnp.bfloat16).reshape(-1, attn)
    cross_term = jnp.dot(crossed, out_cross, preferred_element_type=jnp.float32)
    frames_out = (after_self.astype(jnp.float32) + cross_term).astype(jnp.bfloat16)
    return frames_out.reshape(frame_rows, pixels, width)


MESH = pl.DeviceIdType.MESH
CLIPS, LEVELS, CORES = 4, 4, 2


def greet(peers):
    barrier = pltpu.get_barrier_semaphore()
    for peer in peers:
        pl.semaphore_signal(barrier, inc=1, device_id=peer, device_id_type=MESH)
    pl.semaphore_wait(barrier, len(peers))


def places():
    clip, seq = lax.axis_index("clip"), lax.axis_index("seq")
    level, core = seq // CORES, seq % CORES
    sibling = level * CORES + (1 - core)
    levels = [lax.rem(level + step, LEVELS) for step in range(1, LEVELS)]
    clips = [lax.rem(clip + step, CLIPS) for step in range(1, CLIPS)]
    return clip, seq, level, core, sibling, levels, clips


def remote(src, dst, send_sem, recv_sem, clip, seq):
    return pltpu.make_async_remote_copy(
        src_ref=src,
        dst_ref=dst,
        send_sem=send_sem,
        recv_sem=recv_sem,
        device_id=(clip, seq),
        device_id_type=MESH,
    )


SUBS = ((0, 64), (64, 48))
PROJ_ROWS, OUT_ROWS, QUERY_ROWS = 224, 144, 80
GRANT = 56 * 1024 * 1024


def nt(left, right):
    return lax.dot_general(
        left, right, (((1,), (1,)), ((), ())), preferred_element_type=jnp.float32
    )


def unit(values, axis):
    power = jnp.sum(values * values, axis=axis, keepdims=True) * (1.0 / HEAD_DIM)
    return values * lax.rsqrt(power + EPS)


def project(tokens, weights_ref, qkv_ref):
    per = 3
    for shard in range(weights_ref.shape[0]):
        columns = nt(tokens, weights_ref[shard, :PROJ_ROWS])
        for j in range(per):
            part = columns[:, j * HEAD_DIM : (j + 1) * HEAD_DIM]
            qkv_ref[shard * per + j] = part.astype(jnp.bfloat16)


def self_head(qkv_ref, head, heads, pix):
    rows = qkv_ref.shape[1]
    row = lax.broadcasted_iota(jnp.int32, (rows, rows), 0)
    column = lax.broadcasted_iota(jnp.int32, (rows, rows), 1)
    same = (row % pix) == (column % pix)
    scale_q = 1.0 / math.sqrt(HEAD_DIM)
    query = (unit(qkv_ref[head].astype(jnp.float32), 1) * scale_q).astype(jnp.bfloat16)
    key = unit(qkv_ref[heads + head].astype(jnp.float32), 1).astype(jnp.bfloat16)
    weights = jnp.where(same, jnp.exp(nt(query, key)), 0.0)
    total = jnp.sum(weights, axis=1, keepdims=True)
    mixed = jnp.dot(
        weights.astype(jnp.bfloat16), qkv_ref[2 * heads + head],
        preferred_element_type=jnp.float32,
    )
    return mixed / total


def assemble(weights_ref, out_weight_ref, query_weight_ref):
    outs = PROJ_ROWS + OUT_ROWS
    for src in range(weights_ref.shape[0]):
        out_weight_ref[src * OUT_ROWS : (src + 1) * OUT_ROWS] = weights_ref[src, PROJ_ROWS:outs]
        query_weight_ref[src * QUERY_ROWS : (src + 1) * QUERY_ROWS] = weights_ref[src, outs:]


def sublayers(
    returned_ref, frames_ref, modulation_ref, query_weight_ref, keyval_ref, pick_ref, lengths_ref,
    out_ref, attended_ref, out_weight_ref,
):
    count, block, lanes = returned_ref.shape
    frame_rows, pixels, width = frames_ref.shape
    pix = block // frame_rows
    for src in range(count):
        part = returned_ref[src].astype(jnp.float32)
        for frame in range(frame_rows):
            at = frame * pixels + src * pix
            attended_ref[at : at + pix] = part[frame * pix : (frame + 1) * pix]
    self_term = nt(attended_ref[...].astype(jnp.bfloat16), out_weight_ref[:, :lanes])
    tokens = frames_ref[...].astype(jnp.float32).reshape(frame_rows * pixels, width)
    after_self = (tokens + modulation_ref[2:3] * self_term).astype(jnp.bfloat16)
    text_len = keyval_ref.shape[2]
    live = lax.broadcasted_iota(jnp.int32, (1, text_len), 1) < lengths_ref[pick_ref[0]]
    heads = count
    scale_q = 1.0 / math.sqrt(HEAD_DIM)
    outs = [jnp.zeros((tokens.shape[0], lanes - heads * HEAD_DIM), jnp.float32)]
    per = keyval_ref.shape[1] // HEAD_DIM

    def of_head(index):
        shard = keyval_ref[index // per].astype(jnp.float32)
        return shard[(index % per) * HEAD_DIM : (index % per + 1) * HEAD_DIM]

    queries = nt(after_self, query_weight_ref[...])
    for head in range(heads):
        query = queries[:, head * QUERY_ROWS : head * QUERY_ROWS + HEAD_DIM]
        query = (unit(query, 1) * scale_q).astype(jnp.bfloat16)
        key = unit(of_head(head), 0).astype(jnp.bfloat16)
        scores = jnp.dot(query, key, preferred_element_type=jnp.float32)
        weights = jnp.where(live, jnp.exp(scores), 0.0)
        total = jnp.sum(weights, axis=1, keepdims=True)
        value = of_head(heads + head).astype(jnp.bfloat16)
        outs.append(nt(weights.astype(jnp.bfloat16), value) / total)
    crossed = jnp.concatenate(outs, axis=1).astype(jnp.bfloat16)
    cross_term = nt(crossed, out_weight_ref[:, width - lanes :])
    result = (after_self.astype(jnp.float32) + cross_term).astype(jnp.bfloat16)
    out_ref[...] = result.reshape(frame_rows, pixels, width)


def block_kernel(
    frames_ref, modulation_ref, pack_ref, memory_ref, mask_ref, text_weight_ref,
    pick_ref, lengths_ref,
    out_ref,
    tokens_ref, weights_ref, text_ref, qkv_ref, mixed_ref, returned_ref, columns_ref, keyval_ref,
    attended_ref, out_weight_ref, query_weight_ref,
    normed_ref, blocks_ref, masked_ref, half_ref, held_ref, slots_ref, own_ref,
    block_send, block_recv, pack_send, pack_recv, local_sem, half_sem,
    slice_send, slice_recv, text_send, text_recv,
    back_send, back_recv, keyval_send, keyval_recv,
):
    clip, seq, level, core, sibling, levels, _ = places()
    peers = [lax.rem(seq + step, LEVELS * CORES) for step in range(1, LEVELS * CORES)]
    beside, across, diagonal = clip + 1 - 2 * (clip % 2), (clip + 2) % 4, 3 - clip
    greet([(clip, peer) for peer in peers] + [(beside, seq), (across, seq)])
    pieces = [clip, beside, across, diagonal]
    sends = []

    def rows(part, sub):
        first, size = SUBS[sub]
        return pl.ds(pl.multiple_of(CLIPS * first + part * size, 16), size)

    def start(copy):
        copy.start()
        sends.append(copy)

    def weight(src, shard, part, sub, kind, other, to_clip, to_seq):
        return remote(
            src.at[rows(part, sub)], weights_ref.at[shard, rows(part, sub)],
            pack_send.at[sub, kind, other], pack_recv.at[sub, shard, part], to_clip, to_seq,
        )

    def arrived(shard, part, sub):
        view = weights_ref.at[shard, rows(part, sub)]
        pltpu.make_async_copy(view, view, pack_recv.at[sub, shard, part]).wait()

    def up(sub, source):
        return weight(
            pack_ref if source is None else weights_ref.at[source * CORES + core],
            seq if source is None else source * CORES + core, clip, sub, 0,
            level if source is None else source, clip, jnp.minimum(seq + CORES, LEVELS * CORES - 1),
        )

    def down(sub, source):
        return weight(
            pack_ref if source is None else weights_ref.at[source * CORES + core],
            seq if source is None else source * CORES + core, clip, sub, 1,
            level if source is None else source, clip, jnp.maximum(seq - CORES, 0),
        )

    def climb(sub, source, act):
        upward = level < LEVELS - 1
        downward = level > 0
        if source is not None:
            upward = jnp.logical_and(upward, source < level)
            downward = jnp.logical_and(downward, source > level)

        @pl.when(upward)
        def _():
            act(up(sub, source))

        @pl.when(downward)
        def _():
            act(down(sub, source))

    def spread(sub, source):
        shard = source * CORES + core
        src = weights_ref.at[shard]
        return [
            weight(src, shard, clip, sub, 2, source, beside, seq),
            weight(src, shard, clip, sub, 3, source, across, seq),
            weight(src, shard, clip, sub, 4, source, clip, sibling),
        ]

    def turn(sub, source):
        shard = source * CORES + core
        part, to = (across, beside) if sub == 0 else (beside, across)
        arrived(shard, part, sub)
        start(weight(weights_ref.at[shard], shard, part, sub, 5, source, to, seq))

    def pass_on(sub, source, part, kind):
        shard = source * CORES + core
        start(weight(weights_ref.at[shard], shard, part, sub, kind, source, clip, sibling))

    climb(0, None, lambda copy: copy.start())
    local = [pltpu.make_async_copy(pack_ref, weights_ref.at[seq], local_sem.at[0])]
    local[0].start()

    masked_ref[...] = memory_ref[...] * mask_ref[...]
    half = held_ref.shape[0]
    swap = remote(
        masked_ref.at[pl.ds(pl.multiple_of((1 - core) * half, 16), half)], half_ref,
        half_sem.at[0], half_sem.at[1], clip, sibling,
    )
    start(swap)

    def to_sibling(sub):
        for n, part in enumerate(pieces):
            start(weight(pack_ref, seq, part, sub, 2 + n, level, clip, sibling))

    to_sibling(0)

    def step(sub, distance):
        for source, there in (
            (level - distance, level >= distance),
            (level + distance, level + distance < LEVELS),
        ):

            @pl.when(there)
            def _(source=source):
                arrived(source * CORES + core, clip, sub)
                climb(sub, source, lambda copy: copy.start())
                for copy in spread(sub, source):
                    copy.start()

    frame_rows, pixels, width = frames_ref.shape
    gain, shift = 1.0 + modulation_ref[1:2], modulation_ref[0:1]
    for frame in range(frame_rows):
        normed_ref[frame] = layer_norm(frames_ref[frame].astype(jnp.float32)) * gain + shift
    count = blocks_ref.shape[0]
    pix = pixels // count
    for to in range(count):
        block = normed_ref[:, to * pix : (to + 1) * pix].reshape(frame_rows * pix, width)
        blocks_ref[to] = block.astype(jnp.bfloat16)
    step(0, 1)
    local.append(pltpu.make_async_copy(blocks_ref.at[seq], tokens_ref.at[seq], local_sem.at[1]))
    local[1].start()
    for n, peer in enumerate(peers):
        start(remote(
            blocks_ref.at[peer], tokens_ref.at[seq], block_send.at[n], block_recv.at[seq], clip, peer
        ))

    def text(src, place, index, to):
        start(remote(src, text_ref.at[place], text_send.at[index], text_recv.at[place], clip, to))

    def wait(ref, sem, place):
        pltpu.make_async_copy(ref.at[place], ref.at[place], sem.at[place]).wait()

    step(0, 2)
    step(0, 3)
    climb(1, None, lambda copy: copy.start())
    swap.wait_recv()
    held_ref[...] = masked_ref[pl.ds(pl.multiple_of(core * half, 16), half)] + half_ref[...]
    size = half // LEVELS
    for n, other in enumerate(levels):
        start(remote(
            held_ref.at[pl.ds(pl.multiple_of(other * size, 16), size)], slots_ref.at[level],
            slice_send.at[n], slice_recv.at[level], clip, other * CORES + core,
        ))

    def turn_all(sub):
        for source in levels:
            turn(sub, source)

    def beside_all(sub):
        turned, plain = (across, beside) if sub == 0 else (beside, across)
        for source in levels:
            pass_on(sub, source, turned, 6)
            arrived(source * CORES + core, plain, sub)
            pass_on(sub, source, plain, 7)

    def diagonal_all(sub):
        for source in levels:
            arrived(source * CORES + core, diagonal, sub)
            pass_on(sub, source, diagonal, 8)

    def complete(sub):
        for other in [level] + levels:
            for part in pieces:
                arrived(other * CORES + 1 - core, part, sub)

    turn_all(0)
    beside_all(0)
    step(1, 1)
    diagonal_all(0)
    to_sibling(1)
    total = held_ref[pl.ds(pl.multiple_of(level * size, 16), size)]
    for other in levels:
        wait(slots_ref, slice_recv, other)
        total = total + slots_ref[other]
    own_ref[...] = total
    place = core * LEVELS + level
    local.append(pltpu.make_async_copy(own_ref, text_ref.at[place], local_sem.at[2]))
    local[2].start()
    for n, other in enumerate(levels):
        text(own_ref, place, n, other * CORES + core)
    text(own_ref, place, 3, sibling)

    def keyval(src, shard, index, to):
        start(remote(
            src, keyval_ref.at[shard], keyval_send.at[index], keyval_recv.at[shard], clip, to
        ))

    step(1, 2)
    complete(0)
    step(1, 3)
    for peer in peers:
        wait(tokens_ref, block_recv, peer)
    local[0].wait()
    local[1].wait()
    project(tokens_ref[...].reshape(frame_rows * pixels, width), weights_ref, qkv_ref)
    turn_all(1)
    for n, other in enumerate(levels):
        wait(text_ref, text_recv, core * LEVELS + other)
        text(text_ref.at[core * LEVELS + other], core * LEVELS + other, 4 + n, sibling)
    heads = qkv_ref.shape[0] // 3
    outs = [self_head(qkv_ref, head, heads, pix) for head in range(heads // 2)]
    beside_all(1)
    for other in [level] + levels:
        wait(text_ref, text_recv, (1 - core) * LEVELS + other)
    local[2].wait()
    memory = text_ref[...].reshape(count * text_ref.shape[1], width)
    columns_ref[...] = nt(text_weight_ref[...], memory).astype(jnp.bfloat16)
    local.append(pltpu.make_async_copy(columns_ref, keyval_ref.at[seq], local_sem.at[3]))
    local[3].start()
    for n, other in enumerate(levels):
        keyval(columns_ref, seq, n, other * CORES + core)
    keyval(columns_ref, seq, 3, sibling)
    outs += [self_head(qkv_ref, head, heads, pix) for head in range(heads // 2, heads)]
    lanes = mixed_ref.shape[2]
    outs.append(jnp.zeros((frame_rows * pixels, lanes - heads * HEAD_DIM), jnp.float32))
    mixed = jnp.concatenate(outs, axis=1).astype(jnp.bfloat16)
    mixed_ref[...] = mixed.reshape(mixed_ref.shape)
    local.append(pltpu.make_async_copy(mixed_ref.at[seq], returned_ref.at[seq], local_sem.at[4]))
    local[4].start()
    for n, peer in enumerate(peers):
        start(remote(
            mixed_ref.at[peer], returned_ref.at[seq], back_send.at[n], back_recv.at[seq], clip, peer
        ))
    diagonal_all(1)
    for n, other in enumerate(levels):
        shard = other * CORES + core
        wait(keyval_ref, keyval_recv, shard)
        keyval(keyval_ref.at[shard], shard, 4 + n, sibling)
    complete(1)
    assemble(weights_ref, out_weight_ref, query_weight_ref)
    for other in [level] + levels:
        wait(keyval_ref, keyval_recv, other * CORES + 1 - core)
    for peer in peers:
        wait(returned_ref, back_recv, peer)
    local[3].wait()
    local[4].wait()
    sublayers(
        returned_ref, frames_ref, modulation_ref, query_weight_ref, keyval_ref, pick_ref,
        lengths_ref,
        out_ref, attended_ref, out_weight_ref,
    )
    for sub in range(2):
        climb(sub, None, lambda copy: copy.wait_send())
        for source in levels:
            climb(sub, source, lambda copy: copy.wait_send())
            for copy in spread(sub, source):
                copy.wait_send()
    for copy in sends:
        copy.wait_send()


def whole_block(frames_in, modulation, pack, memory, mask, text_weight, prompt_pick, text_lengths):
    frame_rows, pixels, width = frames_in.shape
    count, kind, text = LEVELS * CORES, frames_in.dtype, memory.shape[0]
    dma, vmem = pltpu.SemaphoreType.DMA, pl.BlockSpec(memory_space=pltpu.VMEM)
    smem = pl.BlockSpec(memory_space=pltpu.SMEM)
    tokens = frame_rows * pixels
    block, size, columns = tokens // count, text // count, text_weight.shape[0]
    heads = count
    lanes = -(-heads * HEAD_DIM // 128) * 128
    return pl.pallas_call(
        block_kernel,
        out_shape=jax.ShapeDtypeStruct(frames_in.shape, kind),
        in_specs=[vmem, vmem, vmem, vmem, vmem, vmem, smem, smem],
        out_specs=vmem,
        scratch_shapes=[
            pltpu.VMEM((count, block, width), kind),
            pltpu.VMEM((count,) + pack.shape, kind),
            pltpu.VMEM((count, size, width), kind),
            pltpu.VMEM((3 * heads, tokens, HEAD_DIM), kind),
            pltpu.VMEM((count, block, lanes), kind),
            pltpu.VMEM((count, block, lanes), kind),
            pltpu.VMEM((columns, text), kind),
            pltpu.VMEM((count, columns, text), kind),
            pltpu.VMEM((tokens, lanes), jnp.float32),
            pltpu.VMEM((count * OUT_ROWS, width), kind),
            pltpu.VMEM((count * QUERY_ROWS, width), kind),
            pltpu.VMEM((frame_rows, pixels, width), jnp.float32),
            pltpu.VMEM((count, block, width), kind),
            pltpu.VMEM((text, width), kind),
            pltpu.VMEM((text // CORES, width), kind),
            pltpu.VMEM((text // CORES, width), kind),
            pltpu.VMEM((LEVELS, size, width), kind),
            pltpu.VMEM((size, width), kind),
            dma((count - 1,)),
            dma((count,)),
            dma((2, 9, LEVELS)),
            dma((2, count, CLIPS)),
            dma((5,)),
            dma((2,)),
            dma((LEVELS - 1,)),
            dma((LEVELS,)),
            dma((7,)),
            dma((count,)),
            dma((count - 1,)),
            dma((count,)),
            dma((7,)),
            dma((count,)),
        ],
        compiler_params=pltpu.CompilerParams(
            collective_id=0, has_side_effects=True, vmem_limit_bytes=GRANT
        ),
    )(frames_in, modulation, pack, memory, mask, text_weight, prompt_pick, text_lengths)


def per_device_shared(
    frames_in,
    modulation,
    self_proj,
    self_out,
    cross_query,
    cross_keyval,
    cross_out,
    text_bank,
    prompt_pick,
    text_lengths,
):
    pick = prompt_pick[0]
    memory = text_bank[0]
    mine = (lax.axis_index("seq") == pick).astype(jnp.bfloat16)
    mask = jnp.full((1, frames_in.shape[2]), mine)

    def fill(part, rows):
        return jnp.pad(part, ((0, rows - part.shape[0]), (0, 0)))

    pack = jnp.concatenate(
        [
            fill(self_proj.T, PROJ_ROWS),
            jnp.concatenate([self_out.T, cross_out.T], axis=1),
            fill(cross_query.T, QUERY_ROWS),
        ],
        axis=0,
    )
    return whole_block(
        frames_in, modulation, pack, memory, mask, cross_keyval.T, prompt_pick, text_lengths
    )


def solution(mesh):
    shared = mesh.shape["clip"] == CLIPS and mesh.shape["seq"] == LEVELS * CORES
    placed = (
        P(("clip", "seq"), None, None),
        P("clip", None),
        P(None, "seq"),
        P(None, "seq"),
        P(None, "seq"),
        P(None, "seq"),
        P(None, "seq"),
        P("seq", None, None),
        P("clip"),
        P(),
    )
    return jax.shard_map(
        per_device_shared if shared else per_device,
        mesh=mesh,
        in_specs=placed,
        out_specs=P(("clip", "seq"), None, None),
        check_vma=False,
    )
```
